128 devices in a mesh: col: 64 (over x, z, y), pw: 2 (over core).
Axes of the slice: x: 4, y: 4, z: 4, core: 2. Of those that a mesh axis runs over, the one named last changes fastest.
Arguments:
- exchange_pairs: bfloat16 [4096, 57344], P('pw', 'col'), may hold values from -0.046875 to 0.046875
- direct_pairs: bfloat16 [4096, 57344], P('pw', 'col'), may hold values from -0.046875 to 0.046875
- test_matrix: bfloat16 [57344, 256], P('col'), may hold values from -6 to 6
- energies: float32 [57344], P('col'), may hold values from 0.8 to 37.5
- picks: int32 [64, 32], P('col'), may hold values from 0 to 895, as said below
Outputs:
- sketch: float32 [2048, 256], P(('col', 'pw'))
- basis: float32 [2048, 256], P(('col', 'pw'))
- factor: float32 [256, 256], replicated
- gram: float32 [256, 256], replicated
The draws below stay inside these ranges and needn't reach their ends.
Inputs may be any that keep to these rules, and one draw needn't show every extreme that they name: `picks`: each row lists 32 distinct local indices of one column block; 0 and 895 are among them.
All inputs are finite; a program needn't handle non-finite values.
Results may differ from the reference program's by a relative error of at most 0.00075.
Values may be sent and summed in bfloat16 or wider, within the bound.
No kernel may reach another device: no remote copies, remote signals or barrier semaphores. Data moves between devices by JAX's collectives and lax.ppermute only.
A program may use at most 128 MiB of HBM per device.

```python
import jax
import jax.numpy as jnp
from jax import lax

G = 4096
COLS_DEV = 896
RANK = 256
ROWS_DEV = 32
NT = 57344
ROWS = 2048
N_COL = 64


def one_block(key):
    first_key, second_key = jax.random.split(key)
    others = jax.random.permutation(first_key, COLS_DEV - 2)[:ROWS_DEV - 2] + 1
    values = jnp.concatenate([jnp.array([0, COLS_DEV - 1], jnp.int32), others.astype(jnp.int32)])
    order = jax.random.permutation(second_key, ROWS_DEV)
    return values[order]


def draw_picks(key, part):
    key = jax.random.fold_in(key, 7)
    keys = jax.random.split(key, N_COL)
    return jax.vmap(one_block)(keys).astype(jnp.int32)


def rising_energies(key, top, low, high):
    where = jnp.arange(NT, dtype=jnp.float32) / jnp.float32(NT - 1)
    base = jnp.exp(jnp.log(jnp.float32(top)) * where)
    rough = jax.random.uniform(key, (NT,), jnp.float32, low, high)
    return base * rough


def draw_energies(key, part):
    key = jax.random.fold_in(key, 11)
    return rising_energies(key, 10.0, 0.8, 1.25).astype(jnp.float32)


def column_scales(key, lowest):
    order_key, jitter_key = jax.random.split(key)
    order = jax.random.permutation(order_key, RANK).astype(jnp.float32)
    jitter = jax.random.uniform(jitter_key, (RANK,), jnp.float32, 0.0, 1.0)
    return jnp.exp(jnp.log(jnp.float32(lowest)) * (order + jitter) / jnp.float32(RANK))


def mixed_columns(shared, spread, scales):
    return shared[:, None] + spread * scales[None, :]


def draw_test_matrix(key, part):
    key = jax.random.fold_in(key, 13)
    scale_key, shared_key, spread_key = jax.random.split(key, 3)
    shared = jnp.clip(jax.random.normal(shared_key, (NT,), jnp.float32), -3.0, 3.0)
    spread = jnp.clip(jax.random.normal(spread_key, (NT, RANK), jnp.float32), -3.0, 3.0)
    scales = column_scales(scale_key, 0.015)
    return mixed_columns(shared, spread, scales).astype(jnp.bfloat16)


def level_of(key, extent, cuts, low, largest):
    gain = 1.0
    for axis_at, parts in cuts:
        heights = jax.random.uniform(jax.random.fold_in(jax.random.fold_in(key, 6), axis_at), (parts,), jnp.float32, low / len(cuts), largest / len(cuts))
        gain = gain * jnp.repeat(jnp.exp(heights), extent[axis_at] // parts).reshape((-1,) + (1,) * (len(extent) - 1 - axis_at))
    return gain


def noise(own_key, shape, scale, reach, pieces=(), held_as=jnp.bfloat16):
    loudness = level_of(own_key, shape, pieces, -0.22, 0.18) if pieces else 1.0
    values = jax.random.normal(own_key, shape, jnp.float32) * scale * loudness
    return jnp.minimum(jnp.maximum(values, -reach), reach).astype(held_as)


def setup_inputs(seed: int = 0) -> dict:
    streams_of = jax.random.split(jax.random.key(seed), 6)
    exchange_pairs = noise(streams_of[0], (G, NT), ((G * NT) ** 0.5) ** -0.5, 0.046875, ((0, 2), (1, 64)))
    direct_pairs = noise(streams_of[1], (G, NT), ((G * NT) ** 0.5) ** -0.5, 0.046875, ((0, 2), (1, 64)))
    test_matrix = draw_test_matrix(jax.random.fold_in(streams_of[5], 71), 0)
    energies = draw_energies(jax.random.fold_in(streams_of[5], 71), 0)
    picks = draw_picks(jax.random.fold_in(streams_of[5], 71), 0)
    return {"exchange_pairs": exchange_pairs, "direct_pairs": direct_pairs, "test_matrix": test_matrix, "energies": energies, "picks": picks}


def orthonormal(matrix):
    gram = jnp.dot(matrix.T, matrix, precision=lax.Precision.HIGHEST)
    lower = jnp.linalg.cholesky(gram)
    result = lax.linalg.triangular_solve(lower, matrix, left_side=False, lower=True, transpose_a=True)
    return (result, lower, gram)

def reference(exchange_pairs, direct_pairs, test_matrix, energies, picks):
    blocks = jnp.arange(N_COL, dtype=jnp.int32)[:, None] * COLS_DEV
    rows = (blocks + picks).reshape(-1).astype(jnp.int32)
    image_x = jnp.dot(exchange_pairs.astype(jnp.float32), test_matrix.astype(jnp.float32), preferred_element_type=jnp.float32)
    image_y = jnp.dot(direct_pairs.astype(jnp.float32), test_matrix.astype(jnp.float32), preferred_element_type=jnp.float32)
    rows_x = jnp.take(exchange_pairs, rows, axis=1).astype(jnp.float32)
    rows_y = jnp.take(direct_pairs, rows, axis=1).astype(jnp.float32)
    coupled = jnp.dot(rows_x.T, 2.0 * image_x, precision=lax.Precision.HIGHEST)
    coupled = coupled - jnp.dot(rows_y.T, image_y, precision=lax.Precision.HIGHEST)
    diagonal = jnp.take(energies, rows)[:, None] * jnp.take(test_matrix, rows, axis=0).astype(jnp.float32)
    sketch = coupled + diagonal
    first, lower1, gram1 = orthonormal(sketch)
    second, lower2, gram2 = orthonormal(first)
    scale = jnp.sqrt(jnp.float32(ROWS))
    basis = second * scale
    factor = jnp.dot(lower2.T, lower1.T, precision=lax.Precision.HIGHEST) / scale
    gram = gram1 / jnp.float32(ROWS)
    return (sketch, basis, factor, gram)
```

```python
import jax
import jax.numpy as jnp
from jax import lax
from jax.experimental import pallas as pl
from jax.experimental.pallas import tpu as pltpu
from jax.sharding import PartitionSpec as P

HIGH = lax.Precision.HIGHEST
F32 = jnp.float32


def dot_lead(left, right):
    return lax.dot_general(left, right, (((0,), (0,)), ((), ())), precision=HIGH, preferred_element_type=F32)


def dot_last(left, right):
    return lax.dot_general(left, right, (((1,), (1,)), ((), ())), precision=HIGH, preferred_element_type=F32)


def splat_lane(tile, lane):
    return jnp.broadcast_to(tile[:, lane:lane + 1], (8, 128))


def splat_row(tile, row):
    return jnp.broadcast_to(tile[row:row + 1, :], (8, 128))


def factor_inverse(work, upper, outer):
    n = work.shape[0]
    tiles = n // 128
    sub = lax.broadcasted_iota(jnp.int32, (8, 128), 0)
    lane = lax.broadcasted_iota(jnp.int32, (8, 128), 1)
    for r0 in range(0, n, outer):
        count = outer // 8
        panel = [[work[r0 + 8 * t:r0 + 8 * t + 8, 128 * c:128 * c + 128] for c in range(tiles)] for t in range(count)]
        for b in range(count):
            r = r0 + 8 * b
            own, base = r // 128, r % 128
            cols = {t: [splat_lane(panel[t][own], base + j) for j in range(8)] for t in range(b, count)}
            d = [[splat_row(cols[b][j], i) if i >= j else None for j in range(8)] for i in range(8)]
            inv = [None] * 8
            low = [[None] * 8 for _ in range(8)]
            for j in range(8):
                inv[j] = lax.rsqrt(d[j][j])
                for i in range(j + 1, 8):
                    low[i][j] = d[i][j] * inv[j]
                for i in range(j + 1, 8):
                    for k in range(j + 1, i + 1):
                        d[i][k] = d[i][k] - low[i][j] * low[k][j]
            mine = (lane >= base) & (lane < base + 8)
            cleared = jnp.where(mine, jnp.where(lane - base == sub, 1.0, 0.0), panel[b][own])
            sources = [panel[b][c] if c != own else cleared for c in range(tiles)] + [panel[b][own]]
            rows = [[splat_row(src, j) for src in sources] for j in range(8)]
            for j in range(8):
                for s in range(tiles + 1):
                    acc = rows[j][s]
                    for k in range(j):
                        acc = acc - low[j][k] * rows[k][s]
                    rows[j][s] = acc * inv[j]
            done = []
            for s in range(tiles + 1):
                tile = rows[0][s]
                for j in range(1, 8):
                    tile = jnp.where(sub == j, rows[j][s], tile)
                done.append(tile)
            for c in range(tiles):
                work[r:r + 8, 128 * c:128 * c + 128] = done[c]
                if c < own:
                    upper[r:r + 8, 128 * c:128 * c + 128] = jnp.zeros((8, 128), F32)
                elif c == own:
                    upper[r:r + 8, 128 * c:128 * c + 128] = jnp.where(lane >= base + sub, done[tiles], 0.0)
                else:
                    upper[r:r + 8, 128 * c:128 * c + 128] = done[c]
            for t in range(b + 1, count):
                below = []
                for j in range(8):
                    acc = cols[t][j]
                    for k in range(j):
                        acc = acc - below[k] * low[j][k]
                    below.append(acc * inv[j])
                for c in range(tiles):
                    acc = panel[t][c]
                    if c == own:
                        acc = jnp.where(mine, 0.0, acc)
                    for j in range(8):
                        acc = acc - below[j] * rows[j][c]
                    panel[t][c] = acc
        after = r0 + outer
        if after < n:
            first_lane = after // 128 * 128
            left = upper[r0:after, first_lane:n]
            done_col = lax.broadcasted_iota(jnp.int32, (outer, n), 1)
            done_row = lax.broadcasted_iota(jnp.int32, (outer, n), 0) + r0
            right = jnp.where((done_col > done_row) & (done_col < after), 0.0, work[r0:after, :])
            change = dot_lead(left, right)
            col = lax.broadcasted_iota(jnp.int32, (n - after, n), 1)
            rest = jnp.where((col >= r0) & (col < after), 0.0, work[after:n, :])
            work[after:n, :] = rest - change[after - first_lane:, :]


def tail_kernel(where_ref, mine_ref, other_ref, basis_ref, factor_ref, gram_ref, held, work, upper, first_upper):
    n = work.shape[0]
    rows = basis_ref.shape[0]
    part = mine_ref.shape[0]
    total = float(2 * part)
    lane = where_ref[0]
    held[pl.ds(pl.multiple_of(lane * part, part), part), :] = mine_ref[...]
    held[pl.ds(pl.multiple_of((1 - lane) * part, part), part), :] = other_ref[...]
    row = lax.broadcasted_iota(jnp.int32, (n, n), 0)
    col = lax.broadcasted_iota(jnp.int32, (n, n), 1)
    gram1 = dot_lead(held[...], held[...])
    gram_ref[...] = gram1 / total
    work[...] = gram1

    def one_pass(step, _):
        factor_inverse(work, upper, 64)
        inverse = jnp.where(col <= row, work[...], 0.0)

        @pl.when(step == 0)
        def _():
            first_upper[...] = upper[...]
            first = dot_last(held[...], inverse)
            held[...] = first
            work[...] = dot_lead(first, first)

        @pl.when(step == 1)
        def _():
            at = pl.multiple_of(where_ref[1], 16)
            basis_ref[...] = dot_last(held[pl.ds(at, rows), :], inverse) * (total ** 0.5)
            factor_ref[...] = jnp.dot(upper[...], first_upper[...], precision=HIGH, preferred_element_type=F32) / (total ** 0.5)

        return 0

    lax.fori_loop(0, 2, one_pass, 0)


def tail(mine, other, where, rows):
    part, n = mine.shape
    vmem = pl.BlockSpec(memory_space=pltpu.VMEM)
    return pl.pallas_call(
        tail_kernel,
        out_shape=(
            jax.ShapeDtypeStruct((rows, n), F32),
            jax.ShapeDtypeStruct((n, n), F32),
            jax.ShapeDtypeStruct((n, n), F32),
        ),
        in_specs=[pl.BlockSpec(memory_space=pltpu.SMEM), vmem, vmem],
        out_specs=(vmem, vmem, vmem),
        scratch_shapes=[
            pltpu.VMEM((2 * part, n), F32),
            pltpu.VMEM((n, n), F32),
            pltpu.VMEM((n, n), F32),
            pltpu.VMEM((n, n), F32),
        ],
        compiler_params=pltpu.CompilerParams(vmem_limit_bytes=48 * 1024 * 1024),
    )(where, mine, other)


def first_kernel(picks_row, picks_col, energy_row, test, left_x, left_y, packed, diagonal, chosen):
    width = test.shape[0]
    block = left_x.shape[0]
    cells = packed.shape[0]
    part = block // cells
    count = picks_col.shape[0]

    @pl.when(pl.program_id(0) == 0)
    def _():
        spot = lax.broadcasted_iota(jnp.int32, (width, 128), 0) == picks_row[...]
        chosen[...] = jnp.where(spot, 1.0, 0.0).astype(jnp.bfloat16)
        here = lax.broadcasted_iota(jnp.int32, (count, width), 1) == picks_col[...]
        energy = jnp.sum(jnp.where(here, energy_row[...], 0.0), axis=1, keepdims=True)
        taken = lax.dot_general(
            here.astype(F32).astype(jnp.bfloat16), test[...], (((1,), (0,)), ((), ())), preferred_element_type=F32
        )
        diagonal[...] = energy * taken

    right = test[...]
    own = []
    for at, (left, weight) in enumerate(((left_x, 2.0), (left_y, -1.0))):
        image = jnp.dot(left[...], right, preferred_element_type=F32) * weight
        packed[:, at * part:(at + 1) * part, :] = image.reshape(cells, part, image.shape[1])
        own.append(jnp.dot(left[...], chosen[...], preferred_element_type=F32).T)
    for cell in range(cells):
        pieces = []
        for group in range(count // 8):
            for rows in own:
                pieces.append(rows[8 * group:8 * group + 8, cell * part:(cell + 1) * part])
        packed[cell, 2 * part:2 * part + 8, :] = jnp.concatenate(pieces, axis=1)


def first_call(exchange, direct, test, energies, picks, cells):
    depth, width = exchange.shape
    rank = test.shape[1]
    count = picks.shape[1]
    part = depth // cells
    block = 256
    per = block // part
    picks_row = jnp.pad(picks, ((0, 0), (0, 128 - count)), constant_values=-1)
    whole = lambda *shape: pl.BlockSpec(shape, lambda i: (0,) * len(shape))
    return pl.pallas_call(
        first_kernel,
        grid=(depth // block,),
        in_specs=[
            whole(1, 128),
            whole(count, 1),
            whole(1, width),
            whole(width, rank),
            pl.BlockSpec((block, width), lambda i: (i, 0)),
            pl.BlockSpec((block, width), lambda i: (i, 0)),
        ],
        out_specs=(
            pl.BlockSpec((per, 2 * part + 8, rank), lambda i: (i, 0, 0)),
            whole(count, rank),
        ),
        out_shape=(
            jax.ShapeDtypeStruct((cells, 2 * part + 8, rank), F32),
            jax.ShapeDtypeStruct((count, rank), F32),
        ),
        scratch_shapes=[pltpu.VMEM((width, 128), jnp.bfloat16)],
        compiler_params=pltpu.CompilerParams(vmem_limit_bytes=32 * 1024 * 1024),
    )(picks_row, picks.reshape(count, 1), energies.reshape(1, width), test, exchange, direct)


def split3(value):
    high = value.astype(jnp.bfloat16)
    rest = value - high.astype(F32)
    middle = rest.astype(jnp.bfloat16)
    low = (rest - middle.astype(F32)).astype(jnp.bfloat16)
    return high, middle, low


def couple_kernel(lane_ref, packed, keep, give):
    cells, height, rank = packed.shape
    depth = height - 8
    image = packed[0, :depth, :]
    for cell in range(1, cells):
        image = image + packed[cell, :depth, :]
    parts = split3(image)
    rows = packed[:, depth:, :].reshape(cells * 8, rank).astype(jnp.bfloat16)
    lane = lane_ref[0]
    for group in range(rank // depth):
        left = rows[:, group * depth:(group + 1) * depth]
        out = jnp.zeros((cells * 8, rank), F32)
        for piece in reversed(parts):
            out = out + jnp.dot(left, piece, preferred_element_type=F32)
        out = out.reshape(cells, 8, rank)
        half, at = group // 2, group % 2 * 8

        @pl.when(lane == half)
        def _():
            keep[:, at:at + 8, :] = out

        @pl.when(lane != half)
        def _():
            give[:, at:at + 8, :] = out


def couple(lane, packed):
    cells, height, rank = packed.shape
    vmem = pl.BlockSpec(memory_space=pltpu.VMEM)
    shape = jax.ShapeDtypeStruct((cells, 16, rank), F32)
    return pl.pallas_call(
        couple_kernel,
        out_shape=(shape, shape),
        in_specs=[pl.BlockSpec(memory_space=pltpu.SMEM), vmem],
        out_specs=(vmem, vmem),
        compiler_params=pltpu.CompilerParams(vmem_limit_bytes=40 * 1024 * 1024),
    )(lane, packed)


SWAP = [(0, 1), (1, 0)]


def shards(exchange_pairs, direct_pairs, test_matrix, energies, picks):
    cells = lax.axis_size("col")
    lane = lax.axis_index("pw")
    place = lax.axis_index("col")
    lane_ref = lane.astype(jnp.int32).reshape(1)
    packed, diagonal = first_call(exchange_pairs, direct_pairs, test_matrix, energies, picks, cells)
    packed = lax.all_to_all(packed, "col", split_axis=0, concat_axis=0, tiled=True)
    keep, give = couple(lane_ref, packed)
    both = keep + lax.ppermute(give, "pw", SWAP)
    arrived = lax.all_to_all(both, "col", split_axis=0, concat_axis=0, tiled=True)
    half = both.shape[1]
    sketch = jnp.sum(arrived, axis=0) + lax.dynamic_slice_in_dim(diagonal, lane * half, half, 0)
    copies = jnp.broadcast_to(sketch[None], (cells,) + sketch.shape)
    mine = lax.all_to_all(copies, "col", split_axis=0, concat_axis=0, tiled=True)
    other = lax.ppermute(mine, "pw", SWAP)
    where = jnp.stack([lane, lane * (cells * half) + place * half]).astype(jnp.int32)
    rank = sketch.shape[1]
    basis, factor, gram = tail(mine.reshape(cells * half, rank), other.reshape(cells * half, rank), where, half)
    return (sketch, basis, factor, gram)


def solution(mesh):
    return jax.shard_map(
        shards,
        mesh=mesh,
        in_specs=(P("pw", "col"), P("pw", "col"), P("col", None), P("col"), P("col", None)),
        out_specs=(P(("col", "pw"), None), P(("col", "pw"), None), P(), P()),
        check_vma=False,
    )
```

```python
import jax
import jax.numpy as jnp
from jax import lax
from jax.experimental import pallas as pl
from jax.experimental.pallas import tpu as pltpu
from jax.sharding import PartitionSpec as P

HIGH = lax.Precision.HIGHEST
F32 = jnp.float32
OUTER = 32


def dot_lead(left, right):
    return lax.dot_general(left, right, (((0,), (0,)), ((), ())), precision=HIGH, preferred_element_type=F32)


def dot_last(left, right):
    return lax.dot_general(left, right, (((1,), (1,)), ((), ())), precision=HIGH, preferred_element_type=F32)


def splat_lane(tile, lane):
    return jnp.broadcast_to(tile[:, lane:lane + 1], (8, 128))


def splat_row(tile, row):
    return jnp.broadcast_to(tile[row:row + 1, :], (8, 128))


def factor_inverse(work, upper, outer):
    n = work.shape[0]
    tiles = n // 128
    sub = lax.broadcasted_iota(jnp.int32, (8, 128), 0)
    lane = lax.broadcasted_iota(jnp.int32, (8, 128), 1)
    for r0 in range(0, n, outer):
        count = outer // 8
        panel = [[work[r0 + 8 * t:r0 + 8 * t + 8, 128 * c:128 * c + 128] for c in range(tiles)] for t in range(count)]
        for b in range(count):
            r = r0 + 8 * b
            own, base = r // 128, r % 128
            cols = {t: [splat_lane(panel[t][own], base + j) for j in range(8)] for t in range(b, count)}
            d = [[splat_row(cols[b][j], i) if i >= j else None for j in range(8)] for i in range(8)]
            inv = [None] * 8
            low = [[None] * 8 for _ in range(8)]
            for j in range(8):
                inv[j] = lax.rsqrt(d[j][j])
                for i in range(j + 1, 8):
                    low[i][j] = d[i][j] * inv[j]
                for i in range(j + 1, 8):
                    for k in range(j + 1, i + 1):
                        d[i][k] = d[i][k] - low[i][j] * low[k][j]
            mine = (lane >= base) & (lane < base + 8)
            cleared = jnp.where(mine, jnp.where(lane - base == sub, 1.0, 0.0), panel[b][own])
            sources = [panel[b][c] if c != own else cleared for c in range(tiles)] + [panel[b][own]]
            rows = [[splat_row(src, j) for src in sources] for j in range(8)]
            for j in range(8):
                for s in range(tiles + 1):
                    acc = rows[j][s]
                    for k in range(j):
                        acc = acc - low[j][k] * rows[k][s]
                    rows[j][s] = acc * inv[j]
            done = []
            for s in range(tiles + 1):
                tile = rows[0][s]
                for j in range(1, 8):
                    tile = jnp.where(sub == j, rows[j][s], tile)
                done.append(tile)
            for c in range(tiles):
                work[r:r + 8, 128 * c:128 * c + 128] = done[c]
                if c < own:
                    upper[r:r + 8, 128 * c:128 * c + 128] = jnp.zeros((8, 128), F32)
                elif c == own:
                    upper[r:r + 8, 128 * c:128 * c + 128] = jnp.where(lane >= base + sub, done[tiles], 0.0)
                else:
                    upper[r:r + 8, 128 * c:128 * c + 128] = done[c]
            for t in range(b + 1, count):
                below = []
                for j in range(8):
                    acc = cols[t][j]
                    for k in range(j):
                        acc = acc - below[k] * low[j][k]
                    below.append(acc * inv[j])
                for c in range(tiles):
                    acc = panel[t][c]
                    if c == own:
                        acc = jnp.where(mine, 0.0, acc)
                    for j in range(8):
                        acc = acc - below[j] * rows[j][c]
                    panel[t][c] = acc
        after = r0 + outer
        if after < n:
            first_lane = after // 128 * 128
            left = upper[r0:after, first_lane:n]
            done_col = lax.broadcasted_iota(jnp.int32, (outer, n), 1)
            done_row = lax.broadcasted_iota(jnp.int32, (outer, n), 0) + r0
            right = jnp.where((done_col > done_row) & (done_col < after), 0.0, work[r0:after, :])
            change = dot_lead(left, right)
            col = lax.broadcasted_iota(jnp.int32, (n - after, n), 1)
            rest = jnp.where((col >= r0) & (col < after), 0.0, work[after:n, :])
            work[after:n, :] = rest - change[after - first_lane:, :]


def split3(value):
    high = value.astype(jnp.bfloat16)
    rest = value - high.astype(F32)
    middle = rest.astype(jnp.bfloat16)
    low = (rest - middle.astype(F32)).astype(jnp.bfloat16)
    return high, middle, low


def dot_bf16(left, right, dims):
    return lax.dot_general(left, right, (dims, ((), ())), preferred_element_type=F32)


def gram_of(parts):
    high, middle, low = parts
    lead = ((0,), (0,))
    cross = dot_bf16(high, middle, lead) + dot_bf16(high, low, lead)
    return dot_bf16(middle, middle, lead) + (cross + cross.T) + dot_bf16(high, high, lead)


def times_transposed(parts, right):
    high, middle, low = parts
    r_high, r_middle, r_low = split3(right)
    left = jnp.concatenate([low, middle, high, middle, high, high], axis=1)
    other = jnp.concatenate([r_high, r_middle, r_low, r_high, r_middle, r_high], axis=1)
    return dot_bf16(left, other, ((1,), (1,)))


def dot_three(left, right, dims):
    l_high, l_middle, _ = split3(left)
    r_high, r_middle, _ = split3(right)
    small = dot_bf16(l_high, r_middle, dims) + dot_bf16(l_middle, r_high, dims)
    return small + dot_bf16(l_high, r_high, dims)


NEAR = 0.0025


def tail_kernel(where_ref, mine_ref, other_ref, basis_ref, factor_ref, gram_ref, held, work, upper, first_upper):
    n = work.shape[0]
    rows = basis_ref.shape[0]
    part = mine_ref.shape[0]
    total = float(2 * part)
    scale = total ** 0.5
    lane = where_ref[0]
    held[pl.ds(pl.multiple_of(lane * part, part), part), :] = mine_ref[...]
    held[pl.ds(pl.multiple_of((1 - lane) * part, part), part), :] = other_ref[...]
    row = lax.broadcasted_iota(jnp.int32, (n, n), 0)
    col = lax.broadcasted_iota(jnp.int32, (n, n), 1)
    identity = jnp.where(row == col, 1.0, 0.0)
    at = pl.multiple_of(where_ref[1], 16)
    gram1 = gram_of(split3(held[...]))
    gram_ref[...] = gram1 / total
    work[...] = gram1

    def one_pass(state):
        step, _ = state
        factor_inverse(work, upper, OUTER)

        def after_first():
            first_upper[...] = upper[...]
            inverse = jnp.where(col <= row, work[...], 0.0)
            first = times_transposed(split3(held[...]), inverse)
            held[...] = first
            gram2 = gram_of(split3(first))
            work[...] = gram2
            error = gram2 - identity
            return jnp.where(jnp.sum(error * error) <= NEAR, 0, 1)

        again = lax.cond(step == 0, after_first, lambda: 0)
        return step + 1, again

    passes, _ = lax.while_loop(lambda state: state[1] > 0, one_pass, (0, 1))

    @pl.when(passes == 1)
    def _():
        error = work[...] - identity
        weight = jnp.where(col < row, 1.0, jnp.where(col == row, 0.5, 0.0))
        extra = error * weight
        for _ in range(2):
            extra = (error - dot_three(extra, extra, ((1,), (1,)))) * weight
        square = dot_three(extra, extra, ((1,), (0,)))
        value = held[pl.ds(at, rows), :]
        value = value - dot_last(value, extra)
        value = value + dot_last(value, square)
        basis_ref[...] = value * scale
        factor_ref[...] = (first_upper[...] + dot_lead(extra, first_upper[...])) / scale

    @pl.when(passes != 1)
    def _():
        inverse = jnp.where(col <= row, work[...], 0.0)
        basis_ref[...] = dot_last(held[pl.ds(at, rows), :], inverse) * scale
        factor_ref[...] = jnp.dot(upper[...], first_upper[...], precision=HIGH, preferred_element_type=F32) / scale


def tail(mine, other, where, rows):
    part, n = mine.shape
    vmem = pl.BlockSpec(memory_space=pltpu.VMEM)
    return pl.pallas_call(
        tail_kernel,
        out_shape=(
            jax.ShapeDtypeStruct((rows, n), F32),
            jax.ShapeDtypeStruct((n, n), F32),
            jax.ShapeDtypeStruct((n, n), F32),
        ),
        in_specs=[pl.BlockSpec(memory_space=pltpu.SMEM), vmem, vmem],
        out_specs=(vmem, vmem, vmem),
        scratch_shapes=[
            pltpu.VMEM((2 * part, n), F32),
            pltpu.VMEM((n, n), F32),
            pltpu.VMEM((n, n), F32),
            pltpu.VMEM((n, n), F32),
        ],
        compiler_params=pltpu.CompilerParams(vmem_limit_bytes=24 * 1024 * 1024),
    )(where, mine, other)


SIDE = 4
STRIDE = {"x": 16, "z": 4, "y": 1}
ORDERS = ("xz", "yx", "zy")
SWAP = [(0, 1), (1, 0)]
STEPS = 4


def whole(*shape):
    return pl.BlockSpec(shape, lambda *_: (0,) * len(shape))


def image_kernel(half, test, x_long, x_short, y_long, y_short, first, second, third):
    short = third.shape[1] // 2

    def image(left, weight, out):
        value = jnp.dot(left[...], test[...], preferred_element_type=F32) * weight
        return value.reshape(out.shape[0], -1, out.shape[2])

    first[...] = image(x_long, 2.0, first)
    second[...] = image(y_long, -1.0, second)
    third[:, :short] = image(x_short, 2.0, third)
    third[:, short:] = image(y_short, -1.0, third)


def image_call(half, exchange, direct, test, room):
    depth, width = exchange.shape
    rank = test.shape[1]
    slices = SIDE * SIDE
    long, short = 3 * depth // (4 * slices), depth // (4 * slices)
    per = slices // 2 // STEPS
    skip = slices * long // (per * short)
    first_block = pl.BlockSpec((per * long, width), lambda i, half: (half[0] * STEPS + i, 0))
    second_block = pl.BlockSpec((per * long, width), lambda i, half: (half[1] * STEPS + i, 0))
    third_block = pl.BlockSpec((per * short, width), lambda i, half: (skip + half[2] * STEPS + i, 0))
    sizes = [long, long, 2 * short]
    return pl.pallas_call(
        image_kernel,
        grid_spec=pltpu.PrefetchScalarGridSpec(
            num_scalar_prefetch=1,
            grid=(STEPS,),
            in_specs=[whole(width, rank), first_block, third_block, second_block, third_block],
            out_specs=[pl.BlockSpec((per, size, rank), lambda i, half: (i, 0, 0)) for size in sizes],
        ),
        out_shape=[jax.ShapeDtypeStruct((slices // 2, size, rank), F32) for size in sizes],
        compiler_params=pltpu.CompilerParams(vmem_limit_bytes=room),
    )(half, test, exchange, exchange, direct, direct)


def rows_kernel(picks_row, picks_col, energy_row, test, x_long, x_short, y_long, y_short, packed, diagonal, chosen, held):
    width = test.shape[0]
    count = picks_col.shape[0]
    long, short = x_long.shape[0] // SIDE, x_short.shape[0] // SIDE
    step = pl.program_id(0)

    @pl.when(step == 0)
    def _():
        spot = lax.broadcasted_iota(jnp.int32, (width, 128), 0) == picks_row[...]
        chosen[...] = jnp.where(spot, 1.0, 0.0).astype(jnp.bfloat16)
        here = lax.broadcasted_iota(jnp.int32, (count, width), 1) == picks_col[...]
        energy = jnp.sum(jnp.where(here, energy_row[...], 0.0), axis=1, keepdims=True)
        taken = jnp.dot(here.astype(F32).astype(jnp.bfloat16), test[...], preferred_element_type=F32)
        diagonal[...] = energy * taken

    def own(left):
        return jnp.dot(left[...], chosen[...], preferred_element_type=F32).T[:count]

    first, second, x_third, y_third = own(x_long), own(y_long), own(x_short), own(y_short)
    blank = lambda size: jnp.zeros((count, size), F32)
    for low in range(SIDE):
        at = step * SIDE + low
        long_cut, short_cut = slice(low * long, (low + 1) * long), slice(low * short, (low + 1) * short)
        held[0, at] = jnp.concatenate([first[:, long_cut], blank(long + 2 * short)], axis=1)
        held[1, at] = jnp.concatenate([blank(long), second[:, long_cut], blank(2 * short)], axis=1)
        held[2, at] = jnp.concatenate([blank(2 * long), x_third[:, short_cut], y_third[:, short_cut]], axis=1)

    @pl.when(step == SIDE - 1)
    def _():
        for x in range(SIDE):
            for z in range(SIDE):
                for y in range(SIDE):
                    cell = x * STRIDE["x"] + z * STRIDE["z"] + y * STRIDE["y"]
                    value = held[0, x * SIDE + z] + held[1, y * SIDE + x] + held[2, z * SIDE + y]
                    packed[cell] = value.astype(jnp.bfloat16)


def rows_call(exchange, direct, test, energies, picks):
    depth, width = exchange.shape
    rank = test.shape[1]
    count = picks.shape[1]
    cells = SIDE ** 3
    slices = SIDE * SIDE
    long, short = 3 * depth // (4 * slices), depth // (4 * slices)
    together = 2 * (long + short)
    picks_row = jnp.pad(picks, ((0, 0), (0, 128 - count)), constant_values=-1)
    long_block = pl.BlockSpec((SIDE * long, width), lambda i: (i, 0))
    short_block = pl.BlockSpec((SIDE * short, width), lambda i: (3 * SIDE + i, 0))
    return pl.pallas_call(
        rows_kernel,
        grid=(SIDE,),
        in_specs=[
            whole(1, 128), whole(count, 1), whole(1, width), whole(width, rank),
            long_block, short_block, long_block, short_block,
        ],
        out_specs=[whole(cells, count, together), whole(count, rank)],
        out_shape=[
            jax.ShapeDtypeStruct((cells, count, together), jnp.bfloat16),
            jax.ShapeDtypeStruct((count, rank), F32),
        ],
        scratch_shapes=[
            pltpu.VMEM((width, 128), jnp.bfloat16),
            pltpu.VMEM((3, slices, count, together), F32),
        ],
        compiler_params=pltpu.CompilerParams(vmem_limit_bytes=56 * 1024 * 1024),
    )(picks_row, picks.reshape(count, 1), energies.reshape(1, width), test, exchange, exchange, direct, direct)


def merge_kernel(bits, *refs):
    kept, came, give, keep = refs[0:3], refs[3:6], refs[6:9], refs[9:12]
    for part in range(3):
        size = give[part].shape[0]
        bit = bits[part]
        away, stay = pl.ds((1 - bit) * size, size), pl.ds(bit * size, size)
        give[part][...] = kept[part][away] + came[part][away]
        keep[part][...] = kept[part][stay] + came[part][stay]


def merge(bits, kept, came):
    vmem = pl.BlockSpec(memory_space=pltpu.VMEM)
    shapes = [jax.ShapeDtypeStruct((k.shape[0] // 2,) + k.shape[1:], F32) for k in kept]
    made = pl.pallas_call(
        merge_kernel,
        out_shape=shapes + shapes,
        in_specs=[pl.BlockSpec(memory_space=pltpu.SMEM)] + [vmem] * 6,
        out_specs=[vmem] * 6,
        compiler_params=pltpu.CompilerParams(vmem_limit_bytes=16 * 1024 * 1024),
    )(bits, *kept, *came)
    return list(made[:3]), list(made[3:])


def couple_kernel(lane_ref, first, second, third, packed, keep, give):
    cells, count, together = packed.shape
    rank = first.shape[-1]
    half_rows = count // 2
    image = jnp.concatenate([first[0], second[0], third[0]], axis=0)
    parts = split3(image)
    lane = lane_ref[0]
    for half in range(2):
        left = packed[:, half * half_rows:(half + 1) * half_rows, :].reshape(cells * half_rows, together)
        out = jnp.zeros((cells * half_rows, rank), F32)
        for piece in reversed(parts):
            out = out + jnp.dot(left, piece, preferred_element_type=F32)
        out = out.reshape(cells, half_rows, rank)

        @pl.when(lane == half)
        def _():
            keep[...] = out

        @pl.when(lane != half)
        def _():
            give[...] = out


def couple(lane, parts, packed):
    cells, count, _ = packed.shape
    rank = parts[0].shape[-1]
    vmem = pl.BlockSpec(memory_space=pltpu.VMEM)
    shape = jax.ShapeDtypeStruct((cells, count // 2, rank), F32)
    return pl.pallas_call(
        couple_kernel,
        out_shape=(shape, shape),
        in_specs=[pl.BlockSpec(memory_space=pltpu.SMEM)] + [vmem] * 4,
        out_specs=(vmem, vmem),
        compiler_params=pltpu.CompilerParams(vmem_limit_bytes=16 * 1024 * 1024),
    )(lane, *parts, packed)


def neighbours(axis, far):
    pairs = []
    for device in range(SIDE ** 3):
        at = device // STRIDE[axis] % SIDE
        to = SIDE - 1 - at if far else at ^ 1
        pairs.append((device, device + (to - at) * STRIDE[axis]))
    return pairs


def shards(exchange_pairs, direct_pairs, test_matrix, energies, picks):
    cells = lax.axis_size("col")
    lane = lax.axis_index("pw")
    place = lax.axis_index("col")
    lane_ref = lane.astype(jnp.int32).reshape(1)
    at = {axis: place // STRIDE[axis] % SIDE for axis in "xyz"}
    far = jnp.stack([at[order[0]] // 2 for order in ORDERS]).astype(jnp.int32)
    near = jnp.stack([at[order[0]] % 2 for order in ORDERS]).astype(jnp.int32)
    gives = image_call(1 - far, exchange_pairs, direct_pairs, test_matrix, 56 * 1024 * 1024)
    picks, gives = lax.optimization_barrier((picks, gives))
    came = [lax.ppermute(give, "col", neighbours(order[0], True)) for give, order in zip(gives, ORDERS)]
    packed, diagonal = rows_call(exchange_pairs, direct_pairs, test_matrix, energies, picks)
    far, packed, diagonal = lax.optimization_barrier((far, packed, diagonal))
    keeps = image_call(far, exchange_pairs, direct_pairs, test_matrix, 56 * 1024 * 1024)
    packed = lax.all_to_all(packed, "col", split_axis=0, concat_axis=0, tiled=True)
    gives, keeps = merge(near, keeps, came)
    for step in range(1, 4):
        if step > 1:
            for part, order in enumerate(ORDERS):
                size = keeps[part].shape[0] // 2
                coordinate = at[order[1]]
                bit = coordinate // 2 if step == 2 else coordinate % 2
                value = keeps[part]
                gives[part] = lax.dynamic_slice_in_dim(value, (1 - bit) * size, size, 0)
                keeps[part] = lax.dynamic_slice_in_dim(value, bit * size, size, 0)
        if step == 2:
            gives, packed, diagonal = lax.optimization_barrier((gives, packed, diagonal))
        else:
            gives = lax.optimization_barrier(gives)
        gives = list(gives)
        for part, order in enumerate(ORDERS):
            keeps[part] = keeps[part] + lax.ppermute(gives[part], "col", neighbours(order[step // 2], step % 2 == 0))
    keep, give = couple(lane_ref, keeps, packed)
    both = keep + lax.ppermute(give, "pw", SWAP)
    half = both.shape[1]
    own_diagonal = lax.dynamic_slice_in_dim(diagonal, lane * half, half, 0)
    where = jnp.stack([lane, lane * (cells * half) + place * half]).astype(jnp.int32)
    both, own_diagonal, where = lax.optimization_barrier((both, own_diagonal, where))
    arrived = lax.all_to_all(both, "col", split_axis=0, concat_axis=0, tiled=True)
    sketch = jnp.sum(arrived, axis=0) + own_diagonal
    copies = jnp.broadcast_to(sketch[None], (cells,) + sketch.shape)
    mine = lax.all_to_all(copies, "col", split_axis=0, concat_axis=0, tiled=True)
    other = lax.ppermute(mine, "pw", SWAP)
    rank = sketch.shape[1]
    basis, factor, gram = tail(mine.reshape(cells * half, rank), other.reshape(cells * half, rank), where, half)
    return (sketch, basis, factor, gram)


def solution(mesh):
    return jax.shard_map(
        shards,
        mesh=mesh,
        in_specs=(P("pw", "col"), P("pw", "col"), P("col", None), P("col"), P("col", None)),
        out_specs=(P(("col", "pw"), None), P(("col", "pw"), None), P(), P()),
        check_vma=False,
    )
```

```python
import jax
import jax.numpy as jnp
from jax import lax
from jax.experimental import pallas as pl
from jax.experimental.pallas import tpu as pltpu
from jax.sharding import PartitionSpec as P

HIGH = lax.Precision.HIGHEST
F32 = jnp.float32
OUTER = 32


def dot_lead(left, right):
    return lax.dot_general(left, right, (((0,), (0,)), ((), ())), precision=HIGH, preferred_element_type=F32)


def dot_last(left, right):
    return lax.dot_general(left, right, (((1,), (1,)), ((), ())), precision=HIGH, preferred_element_type=F32)


def splat_lane(tile, lane):
    return jnp.broadcast_to(tile[:, lane:lane + 1], (8, 128))


def splat_row(tile, row):
    return jnp.broadcast_to(tile[row:row + 1, :], (8, 128))


def split3(value):
    high = value.astype(jnp.bfloat16)
    rest = value - high.astype(F32)
    middle = rest.astype(jnp.bfloat16)
    low = (rest - middle.astype(F32)).astype(jnp.bfloat16)
    return high, middle, low


def dot_bf16(left, right, dims):
    return lax.dot_general(left, right, (dims, ((), ())), preferred_element_type=F32)


STACK_A, STACK_B = (0, 0, 0, 1, 1, 2), (0, 1, 2, 0, 1, 0)


def factor_inverse(work, upper, outer):
    n = work.shape[0]
    tiles = n // 128
    count = outer // 8
    sub = lax.broadcasted_iota(jnp.int32, (8, 128), 0)
    lane = lax.broadcasted_iota(jnp.int32, (8, 128), 1)
    here = work[0:outer, :]
    for r0 in range(0, n, outer):
        panel = [[here[8 * t:8 * t + 8, 128 * c:128 * c + 128] for c in range(tiles)] for t in range(count)]
        uppers, lowers = [], []
        for b in range(count):
            r = r0 + 8 * b
            own, base = r // 128, r % 128
            cols = {t: [splat_lane(panel[t][own], base + j) for j in range(8)] for t in range(b, count)}
            d = [[splat_row(cols[b][j], i) if i >= j else None for j in range(8)] for i in range(8)]
            inv = [None] * 8
            low = [[None] * 8 for _ in range(8)]
            for j in range(8):
                inv[j] = lax.rsqrt(d[j][j])
                for i in range(j + 1, 8):
                    low[i][j] = d[i][j] * inv[j]
                for i in range(j + 1, 8):
                    for k in range(j + 1, i + 1):
                        d[i][k] = d[i][k] - low[i][j] * low[k][j]
            mine = (lane >= base) & (lane < base + 8)
            cleared = jnp.where(mine, jnp.where(lane - base == sub, 1.0, 0.0), panel[b][own])
            sources = [panel[b][c] if c != own else cleared for c in range(tiles)] + [panel[b][own]]
            rows = [[splat_row(src, j) for src in sources] for j in range(8)]
            for j in range(8):
                for s in range(tiles + 1):
                    acc = rows[j][s]
                    for k in range(j):
                        acc = acc - low[j][k] * rows[k][s]
                    rows[j][s] = acc * inv[j]
            for t in range(b + 1, count):
                below = []
                for j in range(8):
                    acc = cols[t][j]
                    for k in range(j):
                        acc = acc - below[k] * low[j][k]
                    below.append(acc * inv[j])
                for c in range(tiles):
                    acc = panel[t][c]
                    if c == own:
                        acc = jnp.where(mine, 0.0, acc)
                    for j in range(8):
                        acc = acc - below[j] * rows[j][c]
                    panel[t][c] = acc
            done = []
            for s in range(tiles + 1):
                tile = rows[0][s]
                for j in range(1, 8):
                    tile = jnp.where(sub == j, rows[j][s], tile)
                done.append(tile)
            up, down = [], []
            for c in range(tiles):
                work[r:r + 8, 128 * c:128 * c + 128] = done[c]
                at = lane + 128 * c - r
                if c < own:
                    up.append(jnp.zeros((8, 128), F32))
                elif c == own:
                    up.append(jnp.where(lane >= base + sub, done[tiles], 0.0))
                else:
                    up.append(done[c])
                upper[r:r + 8, 128 * c:128 * c + 128] = up[c]
                down.append(jnp.where((at >= 8) & (at < outer - 8 * b), 0.0, done[c]) if c == own else done[c])
            uppers.append(jnp.concatenate(up, axis=1))
            lowers.append(jnp.concatenate(down, axis=1))
        after = r0 + outer
        if after < n:
            up, down = split3(jnp.concatenate(uppers, axis=0)), split3(jnp.concatenate(lowers, axis=0))
            left = jnp.concatenate([up[k] for k in STACK_A[::-1]], axis=0)
            right = jnp.concatenate([down[k] for k in STACK_B[::-1]], axis=0)
            start = after // 128 * 128

            def left_over(begin, end, first, last):
                change = dot_bf16(left[:, first:last], right, ((0,), (0,)))[begin - first:end - first]
                col = lax.broadcasted_iota(jnp.int32, (end - begin, n), 1)
                return jnp.where((col >= r0) & (col < after), 0.0, work[begin:end, :]) - change

            here = left_over(after, after + outer, start, start + 128)
            if after + outer < n:
                work[after + outer:n, :] = left_over(after + outer, n, start, n)


def gram_of(parts):
    high, middle, low = parts
    lead = ((0,), (0,))
    cross = dot_bf16(high, middle, lead) + dot_bf16(high, low, lead)
    return dot_bf16(middle, middle, lead) + (cross + cross.T) + dot_bf16(high, high, lead)


def times_transposed(parts, right):
    high, middle, low = parts
    r_high, r_middle, r_low = split3(right)
    left = jnp.concatenate([low, middle, high, middle, high, high], axis=1)
    other = jnp.concatenate([r_high, r_middle, r_low, r_high, r_middle, r_high], axis=1)
    return dot_bf16(left, other, ((1,), (1,)))


def dot_three(left, right, dims):
    l_high, l_middle, _ = split3(left)
    r_high, r_middle, _ = split3(right)
    small = dot_bf16(l_high, r_middle, dims) + dot_bf16(l_middle, r_high, dims)
    return small + dot_bf16(l_high, r_high, dims)


NEAR = 0.0025


def tail_kernel(where_ref, mine_ref, other_ref, basis_ref, factor_ref, gram_ref, held, work, upper, first_upper):
    n = work.shape[0]
    rows = basis_ref.shape[0]
    part = mine_ref.shape[0]
    total = float(2 * part)
    scale = total ** 0.5
    lane = where_ref[0]
    held[pl.ds(pl.multiple_of(lane * part, part), part), :] = mine_ref[...]
    held[pl.ds(pl.multiple_of((1 - lane) * part, part), part), :] = other_ref[...]
    row = lax.broadcasted_iota(jnp.int32, (n, n), 0)
    col = lax.broadcasted_iota(jnp.int32, (n, n), 1)
    identity = jnp.where(row == col, 1.0, 0.0)
    at = pl.multiple_of(where_ref[1], 16)
    gram1 = gram_of(split3(held[...]))
    gram_ref[...] = gram1 / total
    work[...] = gram1

    def one_pass(state):
        step, _ = state
        factor_inverse(work, upper, OUTER)

        def after_first():
            first_upper[...] = upper[...]
            inverse = jnp.where(col <= row, work[...], 0.0)
            first = times_transposed(split3(held[...]), inverse)
            held[...] = first
            gram2 = gram_of(split3(first))
            work[...] = gram2
            error = gram2 - identity
            return jnp.where(jnp.sum(error * error) <= NEAR, 0, 1)

        again = lax.cond(step == 0, after_first, lambda: 0)
        return step + 1, again

    passes, _ = lax.while_loop(lambda state: state[1] > 0, one_pass, (0, 1))

    @pl.when(passes == 1)
    def _():
        error = work[...] - identity
        weight = jnp.where(col < row, 1.0, jnp.where(col == row, 0.5, 0.0))
        extra = error * weight
        for _ in range(2):
            extra = (error - dot_three(extra, extra, ((1,), (1,)))) * weight
        square = dot_three(extra, extra, ((1,), (0,)))
        value = held[pl.ds(at, rows), :]
        value = value - dot_last(value, extra)
        value = value + dot_last(value, square)
        basis_ref[...] = value * scale
        factor_ref[...] = (first_upper[...] + dot_lead(extra, first_upper[...])) / scale

    @pl.when(passes != 1)
    def _():
        inverse = jnp.where(col <= row, work[...], 0.0)
        basis_ref[...] = dot_last(held[pl.ds(at, rows), :], inverse) * scale
        factor_ref[...] = jnp.dot(upper[...], first_upper[...], precision=HIGH, preferred_element_type=F32) / scale


def tail(mine, other, where, rows):
    part, n = mine.shape
    vmem = pl.BlockSpec(memory_space=pltpu.VMEM)
    return pl.pallas_call(
        tail_kernel,
        out_shape=(
            jax.ShapeDtypeStruct((rows, n), F32),
            jax.ShapeDtypeStruct((n, n), F32),
            jax.ShapeDtypeStruct((n, n), F32),
        ),
        in_specs=[pl.BlockSpec(memory_space=pltpu.SMEM), vmem, vmem],
        out_specs=(vmem, vmem, vmem),
        scratch_shapes=[
            pltpu.VMEM((2 * part, n), F32),
            pltpu.VMEM((n, n), F32),
            pltpu.VMEM((n, n), F32),
            pltpu.VMEM((n, n), F32),
        ],
        compiler_params=pltpu.CompilerParams(vmem_limit_bytes=24 * 1024 * 1024),
    )(where, mine, other)


SIDE = 4
STRIDE = {"x": 16, "z": 4, "y": 1}
ORDERS = ("xy", "yx", "zy")
SWAP = [(0, 1), (1, 0)]


def whole(*shape):
    return pl.BlockSpec(shape, lambda *_: (0,) * len(shape))


def image_blocks(x_long, x_short, y_long, y_short, test, outs):
    short = outs[2].shape[1] // 2

    def image(left, weight, out):
        value = jnp.dot(left[...], test[...], preferred_element_type=F32) * weight
        return value.reshape(out.shape[0], -1, out.shape[2])

    third = [image(x_short, 2.0, outs[2]), image(y_short, -1.0, outs[2])]
    return image(x_long, 2.0, outs[0]), image(y_long, -1.0, outs[1]), jnp.concatenate(third, axis=1)


def send_kernel(half, test, x_long, x_short, y_long, y_short, *outs):
    for value, out in zip(image_blocks(x_long, x_short, y_long, y_short, test, outs), outs):
        out[...] = value


def keep_kernel(half, test, x_long, x_short, y_long, y_short, *refs):
    came, give, keep = refs[:3], refs[3:6], refs[6:]
    step = pl.program_id(0)
    values = image_blocks(x_long, x_short, y_long, y_short, test, give)
    for part in range(3):
        value = values[part] + came[part][...]

        @pl.when(step < pl.num_programs(0) // 2)
        def _():
            give[part][...] = value

        @pl.when(step >= pl.num_programs(0) // 2)
        def _():
            keep[part][...] = value


def image_call(halves, exchange, direct, test, steps, came=None):
    depth, width = exchange.shape
    rank = test.shape[1]
    slices = SIDE * SIDE
    long, short = 3 * depth // (4 * slices), depth // (4 * slices)
    per = slices // 2 // steps
    skip = slices * long // (per * short)
    middle = steps // 2

    def block(i, halves, part):
        if came is None:
            return i
        near = halves[3 + part]
        return jnp.where(i < middle, (1 - near) * middle + i, near * middle + i - middle)

    def left(rows, part, skip):
        return pl.BlockSpec((rows, width), lambda i, halves: (skip + halves[part] * steps + block(i, halves, part), 0))

    sizes = [long, long, 2 * short]
    in_specs = [
        whole(width, rank), left(per * long, 0, 0), left(per * short, 2, skip),
        left(per * long, 1, 0), left(per * short, 2, skip),
    ]
    operands = [halves, test, exchange, exchange, direct, direct]
    if came is None:
        out_specs = [pl.BlockSpec((per, size, rank), lambda i, halves: (i, 0, 0)) for size in sizes]
        shapes = [(slices // 2, size, rank) for size in sizes]
    else:
        for part, size in enumerate(sizes):
            in_specs.append(pl.BlockSpec(
                (per, size, rank), lambda i, halves, part=part: (block(i, halves, part), 0, 0)
            ))
        operands += came
        out_specs = [
            pl.BlockSpec((per, size, rank), lambda i, halves: (jnp.minimum(i, middle - 1), 0, 0)) for size in sizes
        ] + [
            pl.BlockSpec((per, size, rank), lambda i, halves: (jnp.maximum(i - middle, 0), 0, 0)) for size in sizes
        ]
        shapes = [(slices // 4, size, rank) for size in sizes] * 2
    return list(pl.pallas_call(
        send_kernel if came is None else keep_kernel,
        grid_spec=pltpu.PrefetchScalarGridSpec(
            num_scalar_prefetch=1, grid=(steps,), in_specs=in_specs, out_specs=out_specs
        ),
        out_shape=[jax.ShapeDtypeStruct(shape, F32) for shape in shapes],
        compiler_params=pltpu.CompilerParams(vmem_limit_bytes=56 * 1024 * 1024 if came is None else 56 * 1024 * 1024),
    )(*operands))


def rows_kernel(picks_row, energy_row, test, x_long, x_short, y_long, y_short, packed, diagonal, chosen, held):
    width = test.shape[0]
    count = picks_row.shape[1]
    together = packed.shape[2]
    long, short = 3 * together // 8, together // 8
    per = x_long.shape[0] // long
    step = pl.program_id(0)

    @pl.when(step == 0)
    def _():
        spot = lax.broadcasted_iota(jnp.int32, (width, count), 0) == picks_row[...]
        chosen[...] = jnp.where(spot, 1.0, 0.0).astype(jnp.bfloat16)
        column = jnp.broadcast_to(picks_row[...].astype(F32), (count, count)).T[:, :1].astype(jnp.int32)
        here = lax.broadcasted_iota(jnp.int32, (count, width), 1) == column
        energy = jnp.sum(jnp.where(here, energy_row[...], 0.0), axis=1, keepdims=True)
        taken = jnp.dot(here.astype(F32).astype(jnp.bfloat16), test[...], preferred_element_type=F32)
        diagonal[...] = energy * taken

    def own(left):
        return jnp.dot(left[...], chosen[...], preferred_element_type=F32).T

    first, second, x_third, y_third = own(x_long), own(y_long), own(x_short), own(y_short)
    blank = lambda size: jnp.zeros((count, size), F32)
    for low in range(per):
        at = step * per + low
        long_cut, short_cut = slice(low * long, (low + 1) * long), slice(low * short, (low + 1) * short)
        held[0, at] = jnp.concatenate([first[:, long_cut], blank(long + 2 * short)], axis=1)
        held[1, at] = jnp.concatenate([blank(long + 2 * short), second[:, long_cut]], axis=1)
        held[2, at] = jnp.concatenate(
            [blank(long), x_third[:, short_cut], y_third[:, short_cut], blank(long)], axis=1
        )

    @pl.when(step == pl.num_programs(0) - 1)
    def _():
        for x in range(SIDE):
            for z in range(SIDE):
                for y in range(SIDE):
                    cell = x * STRIDE["x"] + z * STRIDE["z"] + y * STRIDE["y"]
                    value = held[0, x * SIDE + y] + held[1, y * SIDE + x] + held[2, z * SIDE + y]
                    packed[cell] = value.astype(jnp.bfloat16)


def rows_call(exchange, direct, test, energies, picks):
    depth, width = exchange.shape
    rank = test.shape[1]
    count = picks.shape[1]
    cells = SIDE ** 3
    slices = SIDE * SIDE
    long, short = 3 * depth // (4 * slices), depth // (4 * slices)
    together = 2 * (long + short)
    steps = 1
    long_block = pl.BlockSpec((slices // steps * long, width), lambda i: (i, 0))
    short_block = pl.BlockSpec((slices // steps * short, width), lambda i: (3 * steps + i, 0))
    return pl.pallas_call(
        rows_kernel,
        grid=(steps,),
        in_specs=[
            whole(1, count), whole(1, width), whole(width, rank),
            long_block, short_block, long_block, short_block,
        ],
        out_specs=[whole(cells, count, together), whole(count, rank)],
        out_shape=[
            jax.ShapeDtypeStruct((cells, count, together), jnp.bfloat16),
            jax.ShapeDtypeStruct((count, rank), F32),
        ],
        scratch_shapes=[
            pltpu.VMEM((width, count), jnp.bfloat16),
            pltpu.VMEM((3, slices, count, together), F32),
        ],
        compiler_params=pltpu.CompilerParams(vmem_limit_bytes=56 * 1024 * 1024),
    )(picks, energies.reshape(1, width), test, exchange, exchange, direct, direct)


def couple_kernel(first, second, away, own_rows, other_rows, out):
    cells, half_rows, together = own_rows.shape
    image = jnp.concatenate([first[0], second[0]], axis=0)
    total = jnp.zeros((cells * half_rows, image.shape[1]), F32)
    pieces = [(other_rows, piece) for piece in split3(away[...])] + [(own_rows, piece) for piece in split3(image)]
    for rows, piece in (pieces[2], pieces[5], pieces[1], pieces[4], pieces[0], pieces[3]):
        left = rows[...].reshape(cells * half_rows, together)
        total = total + jnp.dot(left, piece, preferred_element_type=F32)
    out[...] = total.reshape(out.shape)


def couple(parts, away, own_rows, other_rows):
    cells, half_rows, _ = own_rows.shape
    vmem = pl.BlockSpec(memory_space=pltpu.VMEM)
    return pl.pallas_call(
        couple_kernel,
        out_shape=jax.ShapeDtypeStruct((cells, half_rows, away.shape[1]), F32),
        in_specs=[vmem] * 5,
        out_specs=vmem,
        compiler_params=pltpu.CompilerParams(vmem_limit_bytes=16 * 1024 * 1024),
    )(*parts, away, own_rows, other_rows)


def neighbours(axis, far):
    pairs = []
    for device in range(SIDE ** 3):
        at = device // STRIDE[axis] % SIDE
        to = SIDE - 1 - at if far else at ^ 1
        pairs.append((device, device + (to - at) * STRIDE[axis]))
    return pairs


def shards(exchange_pairs, direct_pairs, test_matrix, energies, picks):
    cells = lax.axis_size("col")
    lane = lax.axis_index("pw")
    place = lax.axis_index("col")
    at = {axis: place // STRIDE[axis] % SIDE for axis in "xyz"}
    far = jnp.stack([at[order[0]] // 2 for order in ORDERS]).astype(jnp.int32)
    near = jnp.stack([at[order[0]] % 2 for order in ORDERS]).astype(jnp.int32)
    gives = image_call(1 - far, exchange_pairs, direct_pairs, test_matrix, 2)
    picks, gives = lax.optimization_barrier((picks, gives))
    came = [lax.ppermute(give, "col", neighbours(order[0], True)) for give, order in zip(gives, ORDERS)]
    packed, diagonal = rows_call(exchange_pairs, direct_pairs, test_matrix, energies, picks)
    bits, packed, diagonal = lax.optimization_barrier((jnp.concatenate([far, near]), packed, diagonal))
    made = image_call(bits, exchange_pairs, direct_pairs, test_matrix, 2, came)
    packed = lax.all_to_all(packed, "col", split_axis=0, concat_axis=0, tiled=True)
    gives, keeps = lax.optimization_barrier(made[:3]), made[3:]
    keeps = [keep + lax.ppermute(give, "col", neighbours(order[0], False))
             for keep, give, order in zip(keeps, gives, ORDERS)]
    keeps = [jnp.concatenate([keeps[0], keeps[2]], axis=1), keeps[1]]
    for bit_of in (lambda v: v // 2, lambda v: v % 2):
        gives = []
        for part, order in enumerate(ORDERS[:2]):
            value = keeps[part]
            size = value.shape[0] // 2
            bit = bit_of(at[order[1]])
            gives.append(lax.dynamic_slice_in_dim(value, (1 - bit) * size, size, 0))
            keeps[part] = lax.dynamic_slice_in_dim(value, bit * size, size, 0)
        if size > 1:
            gives, packed, diagonal = lax.optimization_barrier((gives, packed, diagonal))
            half = packed.shape[1] // 2
            own_rows = lax.dynamic_slice_in_dim(packed, lane * half, half, 1)
            other_rows = lax.ppermute(lax.dynamic_slice_in_dim(packed, (1 - lane) * half, half, 1), "pw", SWAP)
        else:
            gives = lax.optimization_barrier(gives)
        for part, order in enumerate(ORDERS[:2]):
            keeps[part] = keeps[part] + lax.ppermute(gives[part], "col", neighbours(order[1], size > 1))
    away = lax.ppermute(jnp.concatenate([keep[0] for keep in keeps], axis=0), "pw", SWAP)
    both = couple(keeps, away, own_rows, other_rows)
    own_diagonal = lax.dynamic_slice_in_dim(diagonal, lane * half, half, 0)
    where = jnp.stack([lane, lane * (cells * half) + place * half]).astype(jnp.int32)
    both, own_diagonal, where = lax.optimization_barrier((both, own_diagonal, where))
    arrived = lax.all_to_all(both, "col", split_axis=0, concat_axis=0, tiled=True)
    sketch = jnp.sum(arrived, axis=0) + own_diagonal
    copies = jnp.broadcast_to(sketch[None], (cells,) + sketch.shape)
    mine = lax.all_to_all(copies, "col", split_axis=0, concat_axis=0, tiled=True)
    other = lax.ppermute(mine, "pw", SWAP)
    rank = sketch.shape[1]
    basis, factor, gram = tail(mine.reshape(cells * half, rank), other.reshape(cells * half, rank), where, half)
    return (sketch, basis, factor, gram)


def solution(mesh):
    return jax.shard_map(
        shards,
        mesh=mesh,
        in_specs=(P("pw", "col"), P("pw", "col"), P("col", None), P("col"), P("col", None)),
        out_specs=(P(("col", "pw"), None), P(("col", "pw"), None), P(), P()),
        check_vma=False,
    )
```

```python
import jax
import jax.numpy as jnp
from jax import lax
from jax.experimental import pallas as pl
from jax.experimental.pallas import tpu as pltpu
from jax.sharding import PartitionSpec as P

HIGH = lax.Precision.HIGHEST
F32 = jnp.float32
OUTER = 32


def dot_lead(left, right):
    return lax.dot_general(left, right, (((0,), (0,)), ((), ())), precision=HIGH, preferred_element_type=F32)


def dot_last(left, right):
    return lax.dot_general(left, right, (((1,), (1,)), ((), ())), precision=HIGH, preferred_element_type=F32)


def splat_lane(tile, lane):
    return jnp.broadcast_to(tile[:, lane:lane + 1], (8, 128))


def splat_row(tile, row):
    return jnp.broadcast_to(tile[row:row + 1, :], (8, 128))


def split3(value):
    high = value.astype(jnp.bfloat16)
    rest = value - high.astype(F32)
    middle = rest.astype(jnp.bfloat16)
    low = (rest - middle.astype(F32)).astype(jnp.bfloat16)
    return high, middle, low


def dot_bf16(left, right, dims):
    return lax.dot_general(left, right, (dims, ((), ())), preferred_element_type=F32)


STACK_A, STACK_B = (0, 0, 0, 1, 1, 2), (0, 1, 2, 0, 1, 0)


def factor_inverse(work, upper, outer):
    n = work.shape[0]
    tiles = n // 128
    count = outer // 8
    sub = lax.broadcasted_iota(jnp.int32, (8, 128), 0)
    lane = lax.broadcasted_iota(jnp.int32, (8, 128), 1)
    here = work[0:outer, :]
    for r0 in range(0, n, outer):
        panel = [[here[8 * t:8 * t + 8, 128 * c:128 * c + 128] for c in range(tiles)] for t in range(count)]
        uppers, lowers = [], []
        for b in range(count):
            r = r0 + 8 * b
            own, base = r // 128, r % 128
            cols = {t: [splat_lane(panel[t][own], base + j) for j in range(8)] for t in range(b, count)}
            d = [[splat_row(cols[b][j], i) if i >= j else None for j in range(8)] for i in range(8)]
            inv = [None] * 8
            low = [[None] * 8 for _ in range(8)]
            for j in range(8):
                inv[j] = lax.rsqrt(d[j][j])
                for i in range(j + 1, 8):
                    low[i][j] = d[i][j] * inv[j]
                for i in range(j + 1, 8):
                    for k in range(j + 1, i + 1):
                        d[i][k] = d[i][k] - low[i][j] * low[k][j]
            mine = (lane >= base) & (lane < base + 8)
            cleared = jnp.where(mine, jnp.where(lane - base == sub, 1.0, 0.0), panel[b][own])
            sources = [panel[b][c] if c != own else cleared for c in range(tiles)] + [panel[b][own]]
            rows = [[splat_row(src, j) for src in sources] for j in range(8)]
            for j in range(8):
                for s in range(tiles + 1):
                    acc = rows[j][s]
                    for k in range(j):
                        acc = acc - low[j][k] * rows[k][s]
                    rows[j][s] = acc * inv[j]
            for t in range(b + 1, count):
                below = []
                for j in range(8):
                    acc = cols[t][j]
                    for k in range(j):
                        acc = acc - below[k] * low[j][k]
                    below.append(acc * inv[j])
                for c in range(tiles):
                    acc = panel[t][c]
                    if c == own:
                        acc = jnp.where(mine, 0.0, acc)
                    for j in range(8):
                        acc = acc - below[j] * rows[j][c]
                    panel[t][c] = acc
            done = []
            for s in range(tiles + 1):
                tile = rows[0][s]
                for j in range(1, 8):
                    tile = jnp.where(sub == j, rows[j][s], tile)
                done.append(tile)
            up, down = [], []
            for c in range(tiles):
                work[r:r + 8, 128 * c:128 * c + 128] = done[c]
                at = lane + 128 * c - r
                if c < own:
                    up.append(jnp.zeros((8, 128), F32))
                elif c == own:
                    up.append(jnp.where(lane >= base + sub, done[tiles], 0.0))
                else:
                    up.append(done[c])
                upper[r:r + 8, 128 * c:128 * c + 128] = up[c]
                down.append(jnp.where((at >= 8) & (at < outer - 8 * b), 0.0, done[c]) if c == own else done[c])
            uppers.append(jnp.concatenate(up, axis=1))
            lowers.append(jnp.concatenate(down, axis=1))
        after = r0 + outer
        if after < n:
            up, down = split3(jnp.concatenate(uppers, axis=0)), split3(jnp.concatenate(lowers, axis=0))
            left = jnp.concatenate([up[k] for k in STACK_A[::-1]], axis=0)
            right = jnp.concatenate([down[k] for k in STACK_B[::-1]], axis=0)
            start = after // 128 * 128

            def left_over(begin, end, first, last):
                change = dot_bf16(left[:, first:last], right, ((0,), (0,)))[begin - first:end - first]
                col = lax.broadcasted_iota(jnp.int32, (end - begin, n), 1)
                return jnp.where((col >= r0) & (col < after), 0.0, work[begin:end, :]) - change

            here = left_over(after, after + outer, start, start + 128)
            if after + outer < n:
                work[after + outer:n, :] = left_over(after + outer, n, start, n)


def gram_of(parts):
    high, middle, low = parts
    lead = ((0,), (0,))
    cross = dot_bf16(high, middle, lead) + dot_bf16(high, low, lead)
    return dot_bf16(middle, middle, lead) + (cross + cross.T) + dot_bf16(high, high, lead)


def times_transposed(parts, right):
    high, middle, low = parts
    r_high, r_middle, r_low = split3(right)
    left = jnp.concatenate([low, middle, high, middle, high, high], axis=1)
    other = jnp.concatenate([r_high, r_middle, r_low, r_high, r_middle, r_high], axis=1)
    return dot_bf16(left, other, ((1,), (1,)))


def dot_three(left, right, dims):
    l_high, l_middle, _ = split3(left)
    r_high, r_middle, _ = split3(right)
    small = dot_bf16(l_high, r_middle, dims) + dot_bf16(l_middle, r_high, dims)
    return small + dot_bf16(l_high, r_high, dims)


NEAR = 0.0025


def gram_kernel(value, out):
    out[...] = gram_of(split3(value[...]))


def tail_kernel(where_ref, mine_ref, other_ref, mine_gram, basis_ref, factor_ref, gram_ref, held, work, upper, first_upper):
    n = work.shape[0]
    rows = basis_ref.shape[0]
    part = mine_ref.shape[0]
    total = float(2 * part)
    scale = total ** 0.5
    row = lax.broadcasted_iota(jnp.int32, (n, n), 0)
    col = lax.broadcasted_iota(jnp.int32, (n, n), 1)
    identity = jnp.where(row == col, 1.0, 0.0)
    at = pl.multiple_of(where_ref[0], 16)
    gram1 = mine_gram[...] + gram_of(split3(other_ref[...]))
    gram_ref[...] = gram1 / total
    work[...] = gram1

    def one_pass(state):
        step, _ = state
        factor_inverse(work, upper, OUTER)

        def after_first():
            first_upper[...] = upper[...]
            inverse = jnp.where(col <= row, work[...], 0.0)
            first = times_transposed(split3(mine_ref[...]), inverse)
            held[...] = first
            gram2 = gram_of(split3(first))
            gram2 = gram2 + gram_of(split3(times_transposed(split3(other_ref[...]), inverse)))
            work[...] = gram2
            error = gram2 - identity
            return jnp.where(jnp.sum(error * error) <= NEAR, 0, 1)

        again = lax.cond(step == 0, after_first, lambda: 0)
        return step + 1, again

    passes, _ = lax.while_loop(lambda state: state[1] > 0, one_pass, (0, 1))

    @pl.when(passes == 1)
    def _():
        error = work[...] - identity
        weight = jnp.where(col < row, 1.0, jnp.where(col == row, 0.5, 0.0))
        extra = error * weight
        for _ in range(2):
            extra = (error - dot_three(extra, extra, ((1,), (1,)))) * weight
        square = dot_three(extra, extra, ((1,), (0,)))
        value = held[pl.ds(at, rows), :]
        value = value - dot_last(value, extra)
        value = value + dot_last(value, square)
        basis_ref[...] = value * scale
        factor_ref[...] = (first_upper[...] + dot_lead(extra, first_upper[...])) / scale

    @pl.when(passes != 1)
    def _():
        inverse = jnp.where(col <= row, work[...], 0.0)
        basis_ref[...] = dot_last(held[pl.ds(at, rows), :], inverse) * scale
        factor_ref[...] = jnp.dot(upper[...], first_upper[...], precision=HIGH, preferred_element_type=F32) / scale


def half_gram(mine):
    n = mine.shape[1]
    vmem = pl.BlockSpec(memory_space=pltpu.VMEM)
    return pl.pallas_call(
        gram_kernel,
        out_shape=jax.ShapeDtypeStruct((n, n), F32),
        in_specs=[vmem],
        out_specs=vmem,
        compiler_params=pltpu.CompilerParams(vmem_limit_bytes=16 * 1024 * 1024),
    )(mine)


def tail(mine, other, mine_gram, where, rows):
    part, n = mine.shape
    vmem = pl.BlockSpec(memory_space=pltpu.VMEM)
    return pl.pallas_call(
        tail_kernel,
        out_shape=(
            jax.ShapeDtypeStruct((rows, n), F32),
            jax.ShapeDtypeStruct((n, n), F32),
            jax.ShapeDtypeStruct((n, n), F32),
        ),
        in_specs=[pl.BlockSpec(memory_space=pltpu.SMEM), vmem, vmem, vmem],
        out_specs=(vmem, vmem, vmem),
        scratch_shapes=[
            pltpu.VMEM((part, n), F32),
            pltpu.VMEM((n, n), F32),
            pltpu.VMEM((n, n), F32),
            pltpu.VMEM((n, n), F32),
        ],
        compiler_params=pltpu.CompilerParams(vmem_limit_bytes=24 * 1024 * 1024),
    )(where, mine, other, mine_gram)


SIDE = 4
STRIDE = {"x": 16, "z": 4, "y": 1}
ORDERS = ("xy", "yx", "zy")
SWAP = [(0, 1), (1, 0)]


def whole(*shape):
    return pl.BlockSpec(shape, lambda *_: (0,) * len(shape))


def image_blocks(x_long, x_short, y_long, y_short, test, outs):
    short = outs[2].shape[1] // 2

    def image(left, weight, out):
        value = jnp.dot(left[...], test[...], preferred_element_type=F32) * weight
        return value.reshape(out.shape[0], -1, out.shape[2])

    third = [image(x_short, 2.0, outs[2]), image(y_short, -1.0, outs[2])]
    return image(x_long, 2.0, outs[0]), image(y_long, -1.0, outs[1]), jnp.concatenate(third, axis=1)


def send_kernel(half, test, x_long, x_short, y_long, y_short, *outs):
    for value, out in zip(image_blocks(x_long, x_short, y_long, y_short, test, outs), outs):
        out[...] = value


def keep_kernel(half, test, x_long, x_short, y_long, y_short, *refs):
    came, give, keep = refs[:3], refs[3:6], refs[6:]
    step = pl.program_id(0)
    values = image_blocks(x_long, x_short, y_long, y_short, test, give)
    for part in range(3):
        value = values[part] + came[part][...]

        @pl.when(step < pl.num_programs(0) // 2)
        def _():
            give[part][...] = value

        @pl.when(step >= pl.num_programs(0) // 2)
        def _():
            keep[part][...] = value


def image_call(halves, exchange, direct, test, steps, came=None):
    depth, width = exchange.shape
    rank = test.shape[1]
    slices = SIDE * SIDE
    long, short = 3 * depth // (4 * slices), depth // (4 * slices)
    per = slices // 2 // steps
    skip = slices * long // (per * short)
    middle = steps // 2

    def block(i, halves, part):
        if came is None:
            return i
        near = halves[3 + part]
        return jnp.where(i < middle, (1 - near) * middle + i, near * middle + i - middle)

    def left(rows, part, skip):
        return pl.BlockSpec((rows, width), lambda i, halves: (skip + halves[part] * steps + block(i, halves, part), 0))

    sizes = [long, long, 2 * short]
    in_specs = [
        whole(width, rank), left(per * long, 0, 0), left(per * short, 2, skip),
        left(per * long, 1, 0), left(per * short, 2, skip),
    ]
    operands = [halves, test, exchange, exchange, direct, direct]
    if came is None:
        out_specs = [pl.BlockSpec((per, size, rank), lambda i, halves: (i, 0, 0)) for size in sizes]
        shapes = [(slices // 2, size, rank) for size in sizes]
    else:
        for part, size in enumerate(sizes):
            in_specs.append(pl.BlockSpec(
                (per, size, rank), lambda i, halves, part=part: (block(i, halves, part), 0, 0)
            ))
        operands += came
        out_specs = [
            pl.BlockSpec((per, size, rank), lambda i, halves: (jnp.minimum(i, middle - 1), 0, 0)) for size in sizes
        ] + [
            pl.BlockSpec((per, size, rank), lambda i, halves: (jnp.maximum(i - middle, 0), 0, 0)) for size in sizes
        ]
        shapes = [(slices // 4, size, rank) for size in sizes] * 2
    return list(pl.pallas_call(
        send_kernel if came is None else keep_kernel,
        grid_spec=pltpu.PrefetchScalarGridSpec(
            num_scalar_prefetch=1, grid=(steps,), in_specs=in_specs, out_specs=out_specs
        ),
        out_shape=[jax.ShapeDtypeStruct(shape, F32) for shape in shapes],
        compiler_params=pltpu.CompilerParams(vmem_limit_bytes=56 * 1024 * 1024 if came is None else 56 * 1024 * 1024),
    )(*operands))


def rows_kernel(picks_row, energy_row, test, x_long, x_short, y_long, y_short, packed, diagonal, chosen, held):
    width = test.shape[0]
    count = picks_row.shape[1]
    together = packed.shape[2]
    long, short = 3 * together // 8, together // 8
    per = x_long.shape[0] // long
    step = pl.program_id(0)

    @pl.when(step == 0)
    def _():
        spot = lax.broadcasted_iota(jnp.int32, (width, count), 0) == picks_row[...]
        chosen[...] = jnp.where(spot, 1.0, 0.0).astype(jnp.bfloat16)
        column = jnp.broadcast_to(picks_row[...].astype(F32), (count, count)).T[:, :1].astype(jnp.int32)
        here = lax.broadcasted_iota(jnp.int32, (count, width), 1) == column
        energy = jnp.sum(jnp.where(here, energy_row[...], 0.0), axis=1, keepdims=True)
        taken = jnp.dot(here.astype(F32).astype(jnp.bfloat16), test[...], preferred_element_type=F32)
        diagonal[...] = energy * taken

    def own(left):
        return jnp.dot(left[...], chosen[...], preferred_element_type=F32).T

    first, second, x_third, y_third = own(x_long), own(y_long), own(x_short), own(y_short)
    blank = lambda size: jnp.zeros((count, size), F32)
    for low in range(per):
        at = step * per + low
        long_cut, short_cut = slice(low * long, (low + 1) * long), slice(low * short, (low + 1) * short)
        held[0, at] = jnp.concatenate([first[:, long_cut], blank(long + 2 * short)], axis=1)
        held[1, at] = jnp.concatenate([blank(long + 2 * short), second[:, long_cut]], axis=1)
        held[2, at] = jnp.concatenate(
            [blank(long), x_third[:, short_cut], y_third[:, short_cut], blank(long)], axis=1
        )

    @pl.when(step == pl.num_programs(0) - 1)
    def _():
        for x in range(SIDE):
            for z in range(SIDE):
                for y in range(SIDE):
                    cell = x * STRIDE["x"] + z * STRIDE["z"] + y * STRIDE["y"]
                    value = held[0, x * SIDE + y] + held[1, y * SIDE + x] + held[2, z * SIDE + y]
                    packed[cell] = value.astype(jnp.bfloat16)


def rows_call(exchange, direct, test, energies, picks):
    depth, width = exchange.shape
    rank = test.shape[1]
    count = picks.shape[1]
    cells = SIDE ** 3
    slices = SIDE * SIDE
    long, short = 3 * depth // (4 * slices), depth // (4 * slices)
    together = 2 * (long + short)
    steps = 1
    long_block = pl.BlockSpec((slices // steps * long, width), lambda i: (i, 0))
    short_block = pl.BlockSpec((slices // steps * short, width), lambda i: (3 * steps + i, 0))
    return pl.pallas_call(
        rows_kernel,
        grid=(steps,),
        in_specs=[
            whole(1, count), whole(1, width), whole(width, rank),
            long_block, short_block, long_block, short_block,
        ],
        out_specs=[whole(cells, count, together), whole(count, rank)],
        out_shape=[
            jax.ShapeDtypeStruct((cells, count, together), jnp.bfloat16),
            jax.ShapeDtypeStruct((count, rank), F32),
        ],
        scratch_shapes=[
            pltpu.VMEM((width, count), jnp.bfloat16),
            pltpu.VMEM((3, slices, count, together), F32),
        ],
        compiler_params=pltpu.CompilerParams(vmem_limit_bytes=56 * 1024 * 1024),
    )(picks, energies.reshape(1, width), test, exchange, exchange, direct, direct)


def couple_kernel(first, second, away, own_rows, other_rows, out):
    cells, half_rows, together = own_rows.shape
    image = jnp.concatenate([first[0], second[0]], axis=0)
    total = jnp.zeros((cells * half_rows, image.shape[1]), F32)
    pieces = [(other_rows, piece) for piece in split3(away[...])] + [(own_rows, piece) for piece in split3(image)]
    for rows, piece in (pieces[2], pieces[5], pieces[1], pieces[4], pieces[0], pieces[3]):
        left = rows[...].reshape(cells * half_rows, together)
        total = total + jnp.dot(left, piece, preferred_element_type=F32)
    out[...] = total.reshape(out.shape)


def couple(parts, away, own_rows, other_rows):
    cells, half_rows, _ = own_rows.shape
    vmem = pl.BlockSpec(memory_space=pltpu.VMEM)
    return pl.pallas_call(
        couple_kernel,
        out_shape=jax.ShapeDtypeStruct((cells, half_rows, away.shape[1]), F32),
        in_specs=[vmem] * 5,
        out_specs=vmem,
        compiler_params=pltpu.CompilerParams(vmem_limit_bytes=16 * 1024 * 1024),
    )(*parts, away, own_rows, other_rows)


def neighbours(axis, far):
    pairs = []
    for device in range(SIDE ** 3):
        at = device // STRIDE[axis] % SIDE
        to = SIDE - 1 - at if far else at ^ 1
        pairs.append((device, device + (to - at) * STRIDE[axis]))
    return pairs


def shards(exchange_pairs, direct_pairs, test_matrix, energies, picks):
    cells = lax.axis_size("col")
    lane = lax.axis_index("pw")
    place = lax.axis_index("col")
    at = {axis: place // STRIDE[axis] % SIDE for axis in "xyz"}
    far = jnp.stack([at[order[0]] // 2 for order in ORDERS]).astype(jnp.int32)
    near = jnp.stack([at[order[0]] % 2 for order in ORDERS]).astype(jnp.int32)
    gives = image_call(1 - far, exchange_pairs, direct_pairs, test_matrix, 2)
    picks, gives = lax.optimization_barrier((picks, gives))
    came = [lax.ppermute(give, "col", neighbours(order[0], True)) for give, order in zip(gives, ORDERS)]
    packed, diagonal = rows_call(exchange_pairs, direct_pairs, test_matrix, energies, picks)
    bits, packed, diagonal = lax.optimization_barrier((jnp.concatenate([far, near]), packed, diagonal))
    made = image_call(bits, exchange_pairs, direct_pairs, test_matrix, 2, came)
    packed = lax.all_to_all(packed, "col", split_axis=0, concat_axis=0, tiled=True)
    gives, keeps = lax.optimization_barrier(made[:3]), made[3:]
    keeps = [keep + lax.ppermute(give, "col", neighbours(order[0], False))
             for keep, give, order in zip(keeps, gives, ORDERS)]
    keeps = [jnp.concatenate([keeps[0], keeps[2]], axis=1), keeps[1]]
    for bit_of in (lambda v: v // 2, lambda v: v % 2):
        gives = []
        for part, order in enumerate(ORDERS[:2]):
            value = keeps[part]
            size = value.shape[0] // 2
            bit = bit_of(at[order[1]])
            gives.append(lax.dynamic_slice_in_dim(value, (1 - bit) * size, size, 0))
            keeps[part] = lax.dynamic_slice_in_dim(value, bit * size, size, 0)
        if size > 1:
            gives, packed, diagonal = lax.optimization_barrier((gives, packed, diagonal))
            half = packed.shape[1] // 2
            own_rows = lax.dynamic_slice_in_dim(packed, lane * half, half, 1)
            other_rows = lax.ppermute(lax.dynamic_slice_in_dim(packed, (1 - lane) * half, half, 1), "pw", SWAP)
        else:
            gives = lax.optimization_barrier(gives)
        for part, order in enumerate(ORDERS[:2]):
            keeps[part] = keeps[part] + lax.ppermute(gives[part], "col", neighbours(order[1], size > 1))
    away = lax.ppermute(jnp.concatenate([keep[0] for keep in keeps], axis=0), "pw", SWAP)
    both = couple(keeps, away, own_rows, other_rows)
    own_diagonal = lax.dynamic_slice_in_dim(diagonal, lane * half, half, 0)
    where = (place * half).astype(jnp.int32).reshape(1)
    both, own_diagonal, where = lax.optimization_barrier((both, own_diagonal, where))
    arrived = lax.all_to_all(both, "col", split_axis=0, concat_axis=0, tiled=True)
    sketch = jnp.sum(arrived, axis=0) + own_diagonal
    copies = jnp.broadcast_to(sketch[None], (cells,) + sketch.shape)
    mine = lax.all_to_all(copies, "col", split_axis=0, concat_axis=0, tiled=True)
    other = lax.ppermute(mine, "pw", SWAP)
    rank = sketch.shape[1]
    mine, other = mine.reshape(cells * half, rank), other.reshape(cells * half, rank)
    basis, factor, gram = tail(mine, other, half_gram(mine), where, half)
    return (sketch, basis, factor, gram)


def solution(mesh):
    return jax.shard_map(
        shards,
        mesh=mesh,
        in_specs=(P("pw", "col"), P("pw", "col"), P("col", None), P("col"), P("col", None)),
        out_specs=(P(("col", "pw"), None), P(("col", "pw"), None), P(), P()),
        check_vma=False,
    )
```

```python
import jax
import jax.numpy as jnp
from jax import lax
from jax.experimental import pallas as pl
from jax.experimental.pallas import tpu as pltpu
from jax.sharding import PartitionSpec as P

HIGH = lax.Precision.HIGHEST
F32 = jnp.float32
OUTER = 32


def dot_lead(left, right):
    return lax.dot_general(left, right, (((0,), (0,)), ((), ())), precision=HIGH, preferred_element_type=F32)


def dot_last(left, right):
    return lax.dot_general(left, right, (((1,), (1,)), ((), ())), precision=HIGH, preferred_element_type=F32)


def splat_lane(tile, lane):
    return jnp.broadcast_to(tile[:, lane:lane + 1], (8, 128))


def splat_row(tile, row):
    return jnp.broadcast_to(tile[row:row + 1, :], (8, 128))


def split3(value):
    high = value.astype(jnp.bfloat16)
    rest = value - high.astype(F32)
    middle = rest.astype(jnp.bfloat16)
    low = (rest - middle.astype(F32)).astype(jnp.bfloat16)
    return high, middle, low


def dot_bf16(left, right, dims):
    return lax.dot_general(left, right, (dims, ((), ())), preferred_element_type=F32)


STACK_A, STACK_B = (0, 0, 0, 1, 1, 2), (0, 1, 2, 0, 1, 0)


def factor_inverse(work, upper, outer):
    n = work.shape[0]
    tiles = n // 128
    count = outer // 8
    sub = lax.broadcasted_iota(jnp.int32, (8, 128), 0)
    lane = lax.broadcasted_iota(jnp.int32, (8, 128), 1)
    here = work[0:outer, :]
    for r0 in range(0, n, outer):
        panel = [[here[8 * t:8 * t + 8, 128 * c:128 * c + 128] for c in range(tiles)] for t in range(count)]
        uppers, lowers = [], []
        for b in range(count):
            r = r0 + 8 * b
            own, base = r // 128, r % 128
            cols = {t: [splat_lane(panel[t][own], base + j) for j in range(8)] for t in range(b, count)}
            d = [[splat_row(cols[b][j], i) if i >= j else None for j in range(8)] for i in range(8)]
            inv = [None] * 8
            low = [[None] * 8 for _ in range(8)]
            for j in range(8):
                inv[j] = lax.rsqrt(d[j][j])
                for i in range(j + 1, 8):
                    low[i][j] = d[i][j] * inv[j]
                for i in range(j + 1, 8):
                    for k in range(j + 1, i + 1):
                        d[i][k] = d[i][k] - low[i][j] * low[k][j]
            mine = (lane >= base) & (lane < base + 8)
            cleared = jnp.where(mine, jnp.where(lane - base == sub, 1.0, 0.0), panel[b][own])
            sources = [panel[b][c] if c != own else cleared for c in range(tiles)] + [panel[b][own]]
            rows = [[splat_row(src, j) for src in sources] for j in range(8)]
            for j in range(8):
                for s in range(tiles + 1):
                    acc = rows[j][s]
                    for k in range(j):
                        acc = acc - low[j][k] * rows[k][s]
                    rows[j][s] = acc * inv[j]
            for t in range(b + 1, count):
                below = []
                for j in range(8):
                    acc = cols[t][j]
                    for k in range(j):
                        acc = acc - below[k] * low[j][k]
                    below.append(acc * inv[j])
                for c in range(tiles):
                    acc = panel[t][c]
                    if c == own:
                        acc = jnp.where(mine, 0.0, acc)
                    for j in range(8):
                        acc = acc - below[j] * rows[j][c]
                    panel[t][c] = acc
            done = []
            for s in range(tiles + 1):
                tile = rows[0][s]
                for j in range(1, 8):
                    tile = jnp.where(sub == j, rows[j][s], tile)
                done.append(tile)
            up, down = [], []
            for c in range(tiles):
                work[r:r + 8, 128 * c:128 * c + 128] = done[c]
                at = lane + 128 * c - r
                if c < own:
                    up.append(jnp.zeros((8, 128), F32))
                elif c == own:
                    up.append(jnp.where(lane >= base + sub, done[tiles], 0.0))
                else:
                    up.append(done[c])
                upper[r:r + 8, 128 * c:128 * c + 128] = up[c]
                down.append(jnp.where((at >= 8) & (at < outer - 8 * b), 0.0, done[c]) if c == own else done[c])
            uppers.append(jnp.concatenate(up, axis=1))
            lowers.append(jnp.concatenate(down, axis=1))
        after = r0 + outer
        if after < n:
            up, down = split3(jnp.concatenate(uppers, axis=0)), split3(jnp.concatenate(lowers, axis=0))
            left = jnp.concatenate([up[k] for k in STACK_A[::-1]], axis=0)
            right = jnp.concatenate([down[k] for k in STACK_B[::-1]], axis=0)
            start = after // 128 * 128

            def left_over(begin, end, first, last):
                change = dot_bf16(left[:, first:last], right, ((0,), (0,)))[begin - first:end - first]
                col = lax.broadcasted_iota(jnp.int32, (end - begin, n), 1)
                return jnp.where((col >= r0) & (col < after), 0.0, work[begin:end, :]) - change

            here = left_over(after, after + outer, start, start + 128)
            if after + outer < n:
                work[after + outer:n, :] = left_over(after + outer, n, start, n)


def gram_of(parts):
    high, middle, low = parts
    lead = ((0,), (0,))
    cross = dot_bf16(high, middle, lead) + dot_bf16(high, low, lead)
    return dot_bf16(middle, middle, lead) + (cross + cross.T) + dot_bf16(high, high, lead)


def times_transposed(parts, right):
    high, middle, low = parts
    r_high, r_middle, r_low = split3(right)
    left = jnp.concatenate([low, middle, high, middle, high, high], axis=1)
    other = jnp.concatenate([r_high, r_middle, r_low, r_high, r_middle, r_high], axis=1)
    return dot_bf16(left, other, ((1,), (1,)))


def dot_three(left, right, dims):
    l_high, l_middle, _ = split3(left)
    r_high, r_middle, _ = split3(right)
    small = dot_bf16(l_high, r_middle, dims) + dot_bf16(l_middle, r_high, dims)
    return small + dot_bf16(l_high, r_high, dims)


NEAR = 0.0025


def gram_kernel(value, out):
    out[...] = gram_of(split3(value[...]))


def tail_kernel(where_ref, mine_ref, other_ref, mine_gram, basis_ref, factor_ref, gram_ref, held, work, upper, first_upper):
    n = work.shape[0]
    rows = basis_ref.shape[0]
    part = mine_ref.shape[0]
    total = float(2 * part)
    scale = total ** 0.5
    row = lax.broadcasted_iota(jnp.int32, (n, n), 0)
    col = lax.broadcasted_iota(jnp.int32, (n, n), 1)
    identity = jnp.where(row == col, 1.0, 0.0)
    at = pl.multiple_of(where_ref[0], 16)
    gram1 = mine_gram[...] + gram_of(split3(other_ref[...]))
    gram_ref[...] = gram1 / total
    work[...] = gram1

    def one_pass(state):
        step, _ = state
        factor_inverse(work, upper, OUTER)

        def after_first():
            first_upper[...] = upper[...]
            inverse = jnp.where(col <= row, work[...], 0.0)
            first = times_transposed(split3(mine_ref[...]), inverse)
            held[...] = first
            gram2 = gram_of(split3(first))
            gram2 = gram2 + gram_of(split3(times_transposed(split3(other_ref[...]), inverse)))
            work[...] = gram2
            error = gram2 - identity
            return jnp.where(jnp.sum(error * error) <= NEAR, 0, 1)

        again = lax.cond(step == 0, after_first, lambda: 0)
        return step + 1, again

    passes, _ = lax.while_loop(lambda state: state[1] > 0, one_pass, (0, 1))

    @pl.when(passes == 1)
    def _():
        error = work[...] - identity
        weight = jnp.where(col < row, 1.0, jnp.where(col == row, 0.5, 0.0))
        extra = error * weight
        for _ in range(2):
            extra = (error - dot_three(extra, extra, ((1,), (1,)))) * weight
        square = dot_three(extra, extra, ((1,), (0,)))
        value = held[pl.ds(at, rows), :]
        value = value - dot_last(value, extra)
        value = value + dot_last(value, square)
        basis_ref[...] = value * scale
        factor_ref[...] = (first_upper[...] + dot_lead(extra, first_upper[...])) / scale

    @pl.when(passes != 1)
    def _():
        inverse = jnp.where(col <= row, work[...], 0.0)
        basis_ref[...] = dot_last(held[pl.ds(at, rows), :], inverse) * scale
        factor_ref[...] = jnp.dot(upper[...], first_upper[...], precision=HIGH, preferred_element_type=F32) / scale


def half_gram(mine):
    n = mine.shape[1]
    vmem = pl.BlockSpec(memory_space=pltpu.VMEM)
    return pl.pallas_call(
        gram_kernel,
        out_shape=jax.ShapeDtypeStruct((n, n), F32),
        in_specs=[vmem],
        out_specs=vmem,
        compiler_params=pltpu.CompilerParams(vmem_limit_bytes=16 * 1024 * 1024),
    )(mine)


def tail(mine, other, mine_gram, where, rows):
    part, n = mine.shape
    vmem = pl.BlockSpec(memory_space=pltpu.VMEM)
    return pl.pallas_call(
        tail_kernel,
        out_shape=(
            jax.ShapeDtypeStruct((rows, n), F32),
            jax.ShapeDtypeStruct((n, n), F32),
            jax.ShapeDtypeStruct((n, n), F32),
        ),
        in_specs=[pl.BlockSpec(memory_space=pltpu.SMEM), vmem, vmem, vmem],
        out_specs=(vmem, vmem, vmem),
        scratch_shapes=[
            pltpu.VMEM((part, n), F32),
            pltpu.VMEM((n, n), F32),
            pltpu.VMEM((n, n), F32),
            pltpu.VMEM((n, n), F32),
        ],
        compiler_params=pltpu.CompilerParams(vmem_limit_bytes=24 * 1024 * 1024),
    )(where, mine, other, mine_gram)


SIDE = 4
STRIDE = {"x": 16, "z": 4, "y": 1}
ORDERS = ("xy", "yx", "zy")
SWAP = [(0, 1), (1, 0)]


def whole(*shape):
    return pl.BlockSpec(shape, lambda *_: (0,) * len(shape))


def image_blocks(x_long, x_short, y_long, y_short, test, outs):
    short = outs[2].shape[1] // 2

    def image(left, weight, out):
        value = jnp.dot(left[...], test[...], preferred_element_type=F32) * weight
        return value.reshape(out.shape[0], -1, out.shape[2])

    third = [image(x_short, 2.0, outs[2]), image(y_short, -1.0, outs[2])]
    return image(x_long, 2.0, outs[0]), image(y_long, -1.0, outs[1]), jnp.concatenate(third, axis=1)


def send_kernel(half, test, x_long, x_short, y_long, y_short, *outs):
    for value, out in zip(image_blocks(x_long, x_short, y_long, y_short, test, outs), outs):
        out[...] = value


def keep_kernel(half, test, x_long, x_short, y_long, y_short, *refs):
    came, give, keep = refs[:3], refs[3:6], refs[6:]
    step = pl.program_id(0)
    values = image_blocks(x_long, x_short, y_long, y_short, test, give)
    for part in range(3):
        value = values[part] + came[part][...]

        @pl.when(step < pl.num_programs(0) // 2)
        def _():
            give[part][...] = value

        @pl.when(step >= pl.num_programs(0) // 2)
        def _():
            keep[part][...] = value


def image_call(halves, exchange, direct, test, steps, came=None):
    depth, width = exchange.shape
    rank = test.shape[1]
    slices = SIDE * SIDE
    long, short = 3 * depth // (4 * slices), depth // (4 * slices)
    per = slices // 2 // steps
    skip = slices * long // (per * short)
    middle = steps // 2

    def block(i, halves, part):
        if came is None:
            return i
        near = halves[3 + part]
        return jnp.where(i < middle, (1 - near) * middle + i, near * middle + i - middle)

    def left(rows, part, skip):
        return pl.BlockSpec((rows, width), lambda i, halves: (skip + halves[part] * steps + block(i, halves, part), 0))

    sizes = [long, long, 2 * short]
    in_specs = [
        whole(width, rank), left(per * long, 0, 0), left(per * short, 2, skip),
        left(per * long, 1, 0), left(per * short, 2, skip),
    ]
    operands = [halves, test, exchange, exchange, direct, direct]
    if came is None:
        out_specs = [pl.BlockSpec((per, size, rank), lambda i, halves: (i, 0, 0)) for size in sizes]
        shapes = [(slices // 2, size, rank) for size in sizes]
    else:
        for part, size in enumerate(sizes):
            in_specs.append(pl.BlockSpec(
                (per, size, rank), lambda i, halves, part=part: (block(i, halves, part), 0, 0)
            ))
        operands += came
        out_specs = [
            pl.BlockSpec((per, size, rank), lambda i, halves: (jnp.minimum(i, middle - 1), 0, 0)) for size in sizes
        ] + [
            pl.BlockSpec((per, size, rank), lambda i, halves: (jnp.maximum(i - middle, 0), 0, 0)) for size in sizes
        ]
        shapes = [(slices // 4, size, rank) for size in sizes] * 2
    return list(pl.pallas_call(
        send_kernel if came is None else keep_kernel,
        grid_spec=pltpu.PrefetchScalarGridSpec(
            num_scalar_prefetch=1, grid=(steps,), in_specs=in_specs, out_specs=out_specs
        ),
        out_shape=[jax.ShapeDtypeStruct(shape, F32) for shape in shapes],
        compiler_params=pltpu.CompilerParams(vmem_limit_bytes=56 * 1024 * 1024 if came is None else 56 * 1024 * 1024),
    )(*operands))


def rows_kernel(picks_row, energy_row, test, x_long, x_short, y_long, y_short, packed, diagonal, chosen, held):
    width = test.shape[0]
    count = picks_row.shape[1]
    together = packed.shape[2]
    long, short = 3 * together // 8, together // 8
    per = x_long.shape[0] // long
    step = pl.program_id(0)

    @pl.when(step == 0)
    def _():
        spot = lax.broadcasted_iota(jnp.int32, (width, count), 0) == picks_row[...]
        chosen[...] = jnp.where(spot, 1.0, 0.0).astype(jnp.bfloat16)
        column = jnp.broadcast_to(picks_row[...].astype(F32), (count, count)).T[:, :1].astype(jnp.int32)
        here = lax.broadcasted_iota(jnp.int32, (count, width), 1) == column
        energy = jnp.sum(jnp.where(here, energy_row[...], 0.0), axis=1, keepdims=True)
        taken = jnp.dot(here.astype(F32).astype(jnp.bfloat16), test[...], preferred_element_type=F32)
        diagonal[...] = energy * taken

    def own(left):
        return jnp.dot(left[...], chosen[...], preferred_element_type=F32).T

    first, second, x_third, y_third = own(x_long), own(y_long), own(x_short), own(y_short)
    blank = lambda size: jnp.zeros((count, size), F32)
    for low in range(per):
        at = step * per + low
        long_cut, short_cut = slice(low * long, (low + 1) * long), slice(low * short, (low + 1) * short)
        held[0, at] = jnp.concatenate([first[:, long_cut], blank(long + 2 * short)], axis=1)
        held[1, at] = jnp.concatenate([blank(long + 2 * short), second[:, long_cut]], axis=1)
        held[2, at] = jnp.concatenate(
            [blank(long), x_third[:, short_cut], y_third[:, short_cut], blank(long)], axis=1
        )

    @pl.when(step == pl.num_programs(0) - 1)
    def _():
        for x in range(SIDE):
            for z in range(SIDE):
                for y in range(SIDE):
                    cell = x * STRIDE["x"] + z * STRIDE["z"] + y * STRIDE["y"]
                    value = held[0, x * SIDE + y] + held[1, y * SIDE + x] + held[2, z * SIDE + y]
                    packed[cell] = value.astype(jnp.bfloat16)


def rows_call(exchange, direct, test, energies, picks):
    depth, width = exchange.shape
    rank = test.shape[1]
    count = picks.shape[1]
    cells = SIDE ** 3
    slices = SIDE * SIDE
    long, short = 3 * depth // (4 * slices), depth // (4 * slices)
    together = 2 * (long + short)
    steps = 1
    long_block = pl.BlockSpec((slices // steps * long, width), lambda i: (i, 0))
    short_block = pl.BlockSpec((slices // steps * short, width), lambda i: (3 * steps + i, 0))
    return pl.pallas_call(
        rows_kernel,
        grid=(steps,),
        in_specs=[
            whole(1, count), whole(1, width), whole(width, rank),
            long_block, short_block, long_block, short_block,
        ],
        out_specs=[whole(cells, count, together), whole(count, rank)],
        out_shape=[
            jax.ShapeDtypeStruct((cells, count, together), jnp.bfloat16),
            jax.ShapeDtypeStruct((count, rank), F32),
        ],
        scratch_shapes=[
            pltpu.VMEM((width, count), jnp.bfloat16),
            pltpu.VMEM((3, slices, count, together), F32),
        ],
        compiler_params=pltpu.CompilerParams(vmem_limit_bytes=24 * 1024 * 1024),
    )(picks, energies.reshape(1, width), test, exchange, exchange, direct, direct)


def couple_kernel(first, second, away, own_rows, other_rows, out):
    cells, half_rows, together = own_rows.shape
    image = jnp.concatenate([first[0], second[0]], axis=0)
    total = jnp.zeros((cells * half_rows, image.shape[1]), F32)
    pieces = [(other_rows, piece) for piece in split3(away[...])] + [(own_rows, piece) for piece in split3(image)]
    for rows, piece in (pieces[2], pieces[5], pieces[1], pieces[4], pieces[0], pieces[3]):
        left = rows[...].reshape(cells * half_rows, together)
        total = total + jnp.dot(left, piece, preferred_element_type=F32)
    out[...] = total.reshape(out.shape)


def couple(parts, away, own_rows, other_rows):
    cells, half_rows, _ = own_rows.shape
    vmem = pl.BlockSpec(memory_space=pltpu.VMEM)
    return pl.pallas_call(
        couple_kernel,
        out_shape=jax.ShapeDtypeStruct((cells, half_rows, away.shape[1]), F32),
        in_specs=[vmem] * 5,
        out_specs=vmem,
        compiler_params=pltpu.CompilerParams(vmem_limit_bytes=16 * 1024 * 1024),
    )(*parts, away, own_rows, other_rows)


def neighbours(axis, far):
    pairs = []
    for device in range(SIDE ** 3):
        at = device // STRIDE[axis] % SIDE
        to = SIDE - 1 - at if far else at ^ 1
        pairs.append((device, device + (to - at) * STRIDE[axis]))
    return pairs


def shards(exchange_pairs, direct_pairs, test_matrix, energies, picks):
    cells = lax.axis_size("col")
    lane = lax.axis_index("pw")
    place = lax.axis_index("col")
    at = {axis: place // STRIDE[axis] % SIDE for axis in "xyz"}
    far = jnp.stack([at[order[0]] // 2 for order in ORDERS]).astype(jnp.int32)
    near = jnp.stack([at[order[0]] % 2 for order in ORDERS]).astype(jnp.int32)
    gives = image_call(1 - far, exchange_pairs, direct_pairs, test_matrix, 2)
    picks, gives = lax.optimization_barrier((picks, gives))
    came = [lax.ppermute(give, "col", neighbours(order[0], True)) for give, order in zip(gives, ORDERS)]
    packed, diagonal = rows_call(exchange_pairs, direct_pairs, test_matrix, energies, picks)
    bits, packed, diagonal = lax.optimization_barrier((jnp.concatenate([far, near]), packed, diagonal))
    made = image_call(bits, exchange_pairs, direct_pairs, test_matrix, 2, came)
    packed = lax.all_to_all(packed, "col", split_axis=0, concat_axis=0, tiled=True)
    gives, keeps = lax.optimization_barrier(made[:3]), made[3:]
    keeps = [keep + lax.ppermute(give, "col", neighbours(order[0], False))
             for keep, give, order in zip(keeps, gives, ORDERS)]
    keeps = [jnp.concatenate([keeps[0], keeps[2]], axis=1), keeps[1]]
    for bit_of in (lambda v: v // 2, lambda v: v % 2):
        gives = []
        for part, order in enumerate(ORDERS[:2]):
            value = keeps[part]
            size = value.shape[0] // 2
            bit = bit_of(at[order[1]])
            gives.append(lax.dynamic_slice_in_dim(value, (1 - bit) * size, size, 0))
            keeps[part] = lax.dynamic_slice_in_dim(value, bit * size, size, 0)
        if size > 1:
            gives, packed, diagonal = lax.optimization_barrier((gives, packed, diagonal))
            half = packed.shape[1] // 2
            own_rows = lax.dynamic_slice_in_dim(packed, lane * half, half, 1)
            other_rows = lax.ppermute(lax.dynamic_slice_in_dim(packed, (1 - lane) * half, half, 1), "pw", SWAP)
        else:
            gives = lax.optimization_barrier(gives)
        for part, order in enumerate(ORDERS[:2]):
            keeps[part] = keeps[part] + lax.ppermute(gives[part], "col", neighbours(order[1], size > 1))
    away = lax.ppermute(jnp.concatenate([keep[0] for keep in keeps], axis=0), "pw", SWAP)
    both = couple(keeps, away, own_rows, other_rows)
    own_diagonal = lax.dynamic_slice_in_dim(diagonal, lane * half, half, 0)
    where = (place * half).astype(jnp.int32).reshape(1)
    both, own_diagonal, where = lax.optimization_barrier((both, own_diagonal, where))
    arrived = lax.all_to_all(both, "col", split_axis=0, concat_axis=0, tiled=True)
    sketch = jnp.sum(arrived, axis=0) + own_diagonal
    copies = jnp.broadcast_to(sketch[None], (cells,) + sketch.shape)
    mine = lax.all_to_all(copies, "col", split_axis=0, concat_axis=0, tiled=True)
    other = lax.ppermute(mine, "pw", SWAP)
    rank = sketch.shape[1]
    mine, other = mine.reshape(cells * half, rank), other.reshape(cells * half, rank)
    basis, factor, gram = tail(mine, other, half_gram(mine), where, half)
    return (sketch, basis, factor, gram)


def solution(mesh):
    return jax.shard_map(
        shards,
        mesh=mesh,
        in_specs=(P("pw", "col"), P("pw", "col"), P("col", None), P("col"), P("col", None)),
        out_specs=(P(("col", "pw"), None), P(("col", "pw"), None), P(), P()),
        check_vma=False,
    )
```
